32 devices in a mesh: ctx: 8 (over z, x), tp: 4 (over y, core).
Axes of the slice: x: 2, y: 2, z: 4, core: 2. Of those that a mesh axis runs over, the one named last changes fastest.
Arguments:
- signal: bfloat16 [4096, 2048], P('tp', 'ctx'), may hold values from -6 to 6
- pre_gate: bfloat16 [4096, 2048], P('tp', 'ctx'), may hold values from -6 to 6
- post_gate: bfloat16 [4096, 2048], P('tp', 'ctx'), may hold values from -6 to 6
- filter_taps: float32 [4096, 2048], P('tp', 'ctx'), may hold values from -0.125 to 0.125
- skip_gain: float32 [4096], P('tp'), may hold values from -4 to 4
- out_weight: bfloat16 [4096, 4096], P('tp'), may hold values from -0.125 to 0.125
Outputs:
- projected: bfloat16 [4096, 2048], P('tp', 'ctx')
The draws below stay inside these ranges and needn't reach their ends.
All inputs are finite; a program needn't handle non-finite values.
Results may differ from the reference program's by a relative error of at most 0.027.
Values may be sent and summed in bfloat16 or wider, within the bound.
A program may use at most 64 MiB of HBM per device.

```python
import jax
import jax.numpy as jnp
from jax import lax

C = 4096
D = 4096
SEQ = 2048
N_TP = 4


def strengthened(entries, key, source, target, parts, factor):
    owner, partner = [(jnp.arange(entries.shape[dim]) // (entries.shape[dim] // parts)).reshape([-1 if axis == dim else 1 for axis in range(entries.ndim)]) for dim in (source, target)]
    chosen = jax.random.permutation(key, parts)[partner]
    strong = (owner == chosen) | (owner == (partner + parts // 2) % parts)
    return jnp.where(strong, factor * entries, entries)


def levels(rng, extent, split, smallest, top_value):
    def one(position, shards_of):
        steps = jax.random.uniform(jax.random.fold_in(jax.random.fold_in(rng, 6), position), (shards_of,), jnp.float32, smallest / len(split), top_value / len(split))
        return jnp.repeat(jnp.exp(steps), extent[position] // shards_of).reshape((-1,) + (1,) * (len(extent) - position - 1))

    loudness = one(*split[0])
    for cut in split[1:]:
        loudness = loudness * one(*cut)
    return loudness


def gaussian(rng, dims, scale, reach, shards=(), held_as=jnp.bfloat16):
    gain = levels(rng, dims, shards, -0.22, 0.18) if shards else 1.0
    drawn = jax.random.normal(rng, dims, jnp.float32) * scale * gain
    return jnp.minimum(jnp.maximum(drawn, -reach), reach).astype(held_as)


def gaussian_with(rng, shape, scale, limit, shards, heavy, kind=jnp.bfloat16):
    entries = scale * jax.random.normal(rng, shape, jnp.float32)
    if shards:
        entries = entries * levels(rng, shape, shards, -0.22, 0.18)
    return jnp.clip(strengthened(entries, jax.random.fold_in(rng, 3), *heavy), -limit, limit).astype(kind)


def setup_inputs(seed: int = 0) -> dict:
    keys = jax.random.split(jax.random.key(seed), 7)
    return {
        "signal": gaussian(keys[0], (C, SEQ), 1.0, 6.0, ((0, 4), (1, 8))),
        "pre_gate": gaussian(keys[1], (C, SEQ), 1.0, 6.0, ((0, 4), (1, 8))),
        "post_gate": gaussian(keys[2], (C, SEQ), 1.0, 6.0, ((0, 4), (1, 8))),
        "filter_taps": gaussian(keys[3], (C, SEQ), SEQ ** -0.5, 0.125, ((0, 4), (1, 8)), jnp.float32),
        "skip_gain": gaussian(keys[4], (C,), 1.0, 4.0, ((0, 4),), jnp.float32),
        "out_weight": gaussian_with(keys[5], (C, D), C ** -0.5, 0.125, ((0, 4),), (0, 1, 4, 2.0)),
    }


def reference(signal, pre_gate, post_gate, filter_taps, skip_gain, out_weight):
    gated_input = signal.astype(jnp.float32) * pre_gate.astype(jnp.float32)
    length = gated_input.shape[1]
    spectra = jnp.fft.rfft(gated_input, n=2 * length, axis=1) * jnp.fft.rfft(filter_taps, n=2 * length, axis=1)
    convolved = jnp.fft.irfft(spectra, n=2 * length, axis=1)[:, :length]
    mixed = (post_gate.astype(jnp.float32) * (convolved + skip_gain[:, None] * gated_input)).astype(jnp.bfloat16)
    width = C // N_TP

    def add_group(group, total):
        start = (group * width).astype(jnp.int32)
        weights = lax.dynamic_slice_in_dim(out_weight, start, width, 0)
        rows = lax.dynamic_slice_in_dim(mixed, start, width, 0)
        term = lax.dot_general(weights, rows, (((0,), (0,)), ((), ())), preferred_element_type=jnp.float32)
        return total + lax.optimization_barrier(term.astype(jnp.bfloat16)).astype(jnp.float32)

    summed = lax.fori_loop(0, N_TP, add_group, jnp.zeros((D, length), jnp.float32))
    return summed.astype(jnp.bfloat16)
```

```python
import functools
import math

import jax
import jax.numpy as jnp
import numpy as np
from jax import lax
from jax.experimental import pallas as pl
from jax.experimental.pallas import tpu as pltpu
from jax.sharding import PartitionSpec as P

f32 = jnp.float32
bf16 = jnp.bfloat16


def freq_tables(blocks, width):
    total = 2 * blocks * width
    place = np.arange(width, dtype=np.int64)
    tables = []
    for k1 in range(blocks + 1):
        angle = (place[:, None] * (k1 + 2 * blocks * place[None, :]) % total) * (2.0 * math.pi / total)
        c, s = np.cos(angle), np.sin(angle)
        tables.append(np.block([[c, -s], [s, c]]))
    return np.stack(tables).astype(jnp.bfloat16)


def weighted(terms):
    total = None
    for coef, part in terms:
        if abs(coef) < 1e-12:
            continue
        value = part if coef == 1.0 else (-part if coef == -1.0 else part * coef)
        total = value if total is None else total + value
    return total


def unit(fn, b, k1, n):
    value = fn(math.pi * (b * k1 % (2 * n)) / n)
    return float(round(value)) if abs(value - round(value)) < 1e-12 else value


def front(n, rows, load, spec):
    width = spec.shape[-1] // 2
    x = [load(b) for b in range(n)]
    even, odd = range(0, n, 2), range(1, n, 2)
    for k1 in range(n // 2 + 1):
        ce = weighted([(unit(math.cos, b, k1, n), x[b]) for b in even])
        co = weighted([(unit(math.cos, b, k1, n), x[b]) for b in odd])
        se = weighted([(unit(math.sin, b, k1, n), x[b]) for b in even])
        so = weighted([(unit(math.sin, b, k1, n), x[b]) for b in odd])
        k2 = n - k1
        if k1 == k2:
            spec[k1, rows, :width] = ce.astype(bf16)
            spec[k1, rows, width:] = (-so).astype(bf16)
            continue
        spec[k1, rows, :width] = (ce + co).astype(bf16)
        spec[k2, rows, :width] = (ce - co).astype(bf16)
        if k1:
            spec[k1, rows, width:] = (-(se + so)).astype(bf16)
            spec[k2, rows, width:] = (se - so).astype(bf16)


def middle(k1, channels, real_only, spec, table, wide):
    width = table.shape[-1] // 2
    depth = width if real_only else 2 * width
    full = jnp.dot(spec[k1, :, :depth], table[k1, :depth, :], preferred_element_type=f32)
    ur, ui = full[:channels, :width], full[:channels, width:]
    hr, hi = full[channels:, :width], full[channels:, width:]
    prod = jnp.concatenate([ur * hr - ui * hi, ur * hi + ui * hr], axis=1).astype(bf16)
    wide[k1, :, :depth] = lax.dot_general(
        prod, table[k1, :depth, :], (((1,), (1,)), ((), ())), preferred_element_type=f32
    )


def back(n, rows, wide, store):
    width = wide.shape[-1] // 2
    scale = 1.0 / (2 * n * width)
    re = [wide[k, rows, :width] for k in range(n + 1)]
    im = [None if k in (0, n) else wide[k, rows, width:] for k in range(n + 1)]
    for parity in (0, 1):
        sign = 1.0 if parity == 0 else -1.0
        reals, imags = [], []
        for k in range(n // 2):
            reals.append(re[k] + re[n - k] if parity == 0 else re[k] - re[n - k])
            imags.append(None if k == 0 else (im[k] - im[n - k] if parity == 0 else im[k] + im[n - k]))
        for b in range(parity, n, 2):
            terms = []
            for k in range(n // 2):
                weight = scale if k == 0 else 2.0 * scale
                terms.append((weight * unit(math.cos, b, k, n), reals[k]))
                if k:
                    terms.append((-weight * unit(math.sin, b, k, n), imags[k]))
            if parity == 0:
                terms.append((2.0 * scale * unit(math.cos, b, n // 2, n), re[n // 2]))
            else:
                terms.append((-2.0 * scale * unit(math.sin, b, n // 2, n), im[n // 2]))
            terms = [(c if abs(c) > 1e-9 * scale else 0.0, v) for c, v in terms]
            store(b, weighted([(c / scale, v) for c, v in terms]) * scale)


ROWS = 16


def conv_kernel(n, x_ref, table, y_ref, spec, wide):
    channels = y_ref.shape[1]

    def front_step(i, _):
        rows = pl.ds(pl.multiple_of(i * ROWS, ROWS), ROWS)
        front(n, rows, lambda b: x_ref[b, rows, :].astype(f32), spec)
        return 0

    lax.fori_loop(0, 2 * channels // ROWS, front_step, 0)
    middle(0, channels, True, spec, table, wide)
    middle(n, channels, True, spec, table, wide)

    def middle_step(k1, _):
        middle(k1, channels, False, spec, table, wide)
        return 0

    lax.fori_loop(1, n, middle_step, 0)

    height = min(ROWS, channels)

    def back_step(i, _):
        rows = pl.ds(pl.multiple_of(i * height, height), height)

        def store(b, value):
            y_ref[b, rows, :] = value.astype(bf16)

        back(n, rows, wide, store)
        return 0

    lax.fori_loop(0, channels // height, back_step, 0)


def per_device(signal, pre_gate, post_gate, filter_taps, skip_gain, out_weight):
    channels_here, tokens_here = signal.shape
    n = lax.axis_size("ctx")
    mine = channels_here // n
    gated_input = signal.astype(f32) * pre_gate.astype(f32)
    stacked = jnp.stack([gated_input.astype(bf16), filter_taps.astype(bf16)])
    stacked = stacked.reshape(2, n, mine, tokens_here).transpose(1, 0, 2, 3).reshape(n, 2 * mine, tokens_here)
    blocks = lax.all_to_all(stacked, "ctx", split_axis=0, concat_axis=0, tiled=True)
    table = jnp.asarray(freq_tables(n, tokens_here))
    conv = pl.pallas_call(
        functools.partial(conv_kernel, n),
        out_shape=jax.ShapeDtypeStruct((n, mine, tokens_here), bf16),
        in_specs=[pl.BlockSpec(memory_space=pltpu.VMEM)] * 2,
        out_specs=pl.BlockSpec(memory_space=pltpu.VMEM),
        scratch_shapes=[
            pltpu.VMEM((n + 1, 2 * mine, 2 * tokens_here), bf16),
            pltpu.VMEM((n + 1, mine, 2 * tokens_here), f32),
        ],
        compiler_params=pltpu.CompilerParams(vmem_limit_bytes=48 * 1024 * 1024),
    )(blocks, table)
    conv = lax.all_to_all(conv, "ctx", split_axis=0, concat_axis=0, tiled=True)
    convolved = conv.reshape(channels_here, tokens_here).astype(f32)
    mixed = (post_gate.astype(f32) * (convolved + skip_gain[:, None] * gated_input)).astype(bf16)
    return lax.psum_scatter(
        lax.dot_general(
            out_weight, mixed, (((0,), (0,)), ((), ())), preferred_element_type=f32
        ).astype(bf16),
        "tp",
        scatter_dimension=0,
        tiled=True,
    )


def solution(mesh):
    return jax.shard_map(
        per_device,
        mesh=mesh,
        in_specs=(
            P("tp", "ctx"),
            P("tp", "ctx"),
            P("tp", "ctx"),
            P("tp", "ctx"),
            P("tp"),
            P("tp", None),
        ),
        out_specs=P("tp", "ctx"),
        check_vma=False,
    )
```

```python
import functools
import math

import jax
import jax.numpy as jnp
import numpy as np
from jax import lax
from jax.experimental import pallas as pl
from jax.experimental.pallas import tpu as pltpu
from jax.sharding import PartitionSpec as P

f32 = jnp.float32
bf16 = jnp.bfloat16


def freq_tables(blocks, width):
    total = 2 * blocks * width
    place = np.arange(width, dtype=np.int64)
    tables = []
    for k1 in range(blocks + 1):
        angle = (place[:, None] * (k1 + 2 * blocks * place[None, :]) % total) * (2.0 * math.pi / total)
        c, s = np.cos(angle), np.sin(angle)
        tables.append(np.block([[c, -s], [s, c]]))
    return np.stack(tables).astype(jnp.bfloat16)


def weighted(terms):
    total = None
    for coef, part in terms:
        if abs(coef) < 1e-12:
            continue
        value = part if coef == 1.0 else (-part if coef == -1.0 else part * coef)
        total = value if total is None else total + value
    return total


def unit(fn, b, k1, n):
    value = fn(math.pi * (b * k1 % (2 * n)) / n)
    return float(round(value)) if abs(value - round(value)) < 1e-12 else value


def front(n, rows, load, spec):
    width = spec.shape[-1] // 2
    x = [load(b) for b in range(n)]
    even, odd = range(0, n, 2), range(1, n, 2)
    for k1 in range(n // 2 + 1):
        ce = weighted([(unit(math.cos, b, k1, n), x[b]) for b in even])
        co = weighted([(unit(math.cos, b, k1, n), x[b]) for b in odd])
        se = weighted([(unit(math.sin, b, k1, n), x[b]) for b in even])
        so = weighted([(unit(math.sin, b, k1, n), x[b]) for b in odd])
        k2 = n - k1
        if k1 == k2:
            spec[k1, rows, :width] = ce.astype(bf16)
            spec[k1, rows, width:] = (-so).astype(bf16)
            continue
        spec[k1, rows, :width] = (ce + co).astype(bf16)
        spec[k2, rows, :width] = (ce - co).astype(bf16)
        if k1:
            spec[k1, rows, width:] = (-(se + so)).astype(bf16)
            spec[k2, rows, width:] = (se - so).astype(bf16)


def middle(k1, channels, real_only, spec, table, wide):
    width = table.shape[-1] // 2
    depth = width if real_only else 2 * width
    full = jnp.dot(spec[k1, :, :depth], table[k1, :depth, :], preferred_element_type=f32)
    ur, ui = full[:channels, :width], full[:channels, width:]
    hr, hi = full[channels:, :width], full[channels:, width:]
    prod = jnp.concatenate([ur * hr - ui * hi, ur * hi + ui * hr], axis=1).astype(bf16)
    wide[k1, :, :depth] = lax.dot_general(
        prod, table[k1, :depth, :], (((1,), (1,)), ((), ())), preferred_element_type=f32
    )


def back(n, rows, wide, store):
    width = wide.shape[-1] // 2
    scale = 1.0 / (2 * n * width)
    re = [wide[k, rows, :width] for k in range(n + 1)]
    im = [None if k in (0, n) else wide[k, rows, width:] for k in range(n + 1)]
    for parity in (0, 1):
        sign = 1.0 if parity == 0 else -1.0
        reals, imags = [], []
        for k in range(n // 2):
            reals.append(re[k] + re[n - k] if parity == 0 else re[k] - re[n - k])
            imags.append(None if k == 0 else (im[k] - im[n - k] if parity == 0 else im[k] + im[n - k]))
        for b in range(parity, n, 2):
            terms = []
            for k in range(n // 2):
                weight = scale if k == 0 else 2.0 * scale
                terms.append((weight * unit(math.cos, b, k, n), reals[k]))
                if k:
                    terms.append((-weight * unit(math.sin, b, k, n), imags[k]))
            if parity == 0:
                terms.append((2.0 * scale * unit(math.cos, b, n // 2, n), re[n // 2]))
            else:
                terms.append((-2.0 * scale * unit(math.sin, b, n // 2, n), im[n // 2]))
            terms = [(c if abs(c) > 1e-9 * scale else 0.0, v) for c, v in terms]
            store(b, weighted([(c / scale, v) for c, v in terms]) * scale)


ROWS = 16


def conv_kernel(n, x_ref, table, y_ref, spec, wide):
    channels = y_ref.shape[1]

    def front_step(i, _):
        rows = pl.ds(pl.multiple_of(i * ROWS, ROWS), ROWS)
        front(n, rows, lambda b: x_ref[b, rows, :].astype(f32), spec)
        return 0

    lax.fori_loop(0, 2 * channels // ROWS, front_step, 0)
    middle(0, channels, True, spec, table, wide)
    middle(n, channels, True, spec, table, wide)

    def middle_step(k1, _):
        middle(k1, channels, False, spec, table, wide)
        return 0

    lax.fori_loop(1, n, middle_step, 0)

    height = min(ROWS, channels)

    def back_step(i, _):
        rows = pl.ds(pl.multiple_of(i * height, height), height)

        def store(b, value):
            y_ref[b, rows, :] = value.astype(bf16)

        back(n, rows, wide, store)
        return 0

    lax.fori_loop(0, channels // height, back_step, 0)


def per_device_generic(signal, pre_gate, post_gate, filter_taps, skip_gain, out_weight):
    channels_here, tokens_here = signal.shape
    n = lax.axis_size("ctx")
    mine = channels_here // n
    gated_input = signal.astype(f32) * pre_gate.astype(f32)
    stacked = jnp.stack([gated_input.astype(bf16), filter_taps.astype(bf16)])
    stacked = stacked.reshape(2, n, mine, tokens_here).transpose(1, 0, 2, 3).reshape(n, 2 * mine, tokens_here)
    blocks = lax.all_to_all(stacked, "ctx", split_axis=0, concat_axis=0, tiled=True)
    table = jnp.asarray(freq_tables(n, tokens_here))
    conv = pl.pallas_call(
        functools.partial(conv_kernel, n),
        out_shape=jax.ShapeDtypeStruct((n, mine, tokens_here), bf16),
        in_specs=[pl.BlockSpec(memory_space=pltpu.VMEM)] * 2,
        out_specs=pl.BlockSpec(memory_space=pltpu.VMEM),
        scratch_shapes=[
            pltpu.VMEM((n + 1, 2 * mine, 2 * tokens_here), bf16),
            pltpu.VMEM((n + 1, mine, 2 * tokens_here), f32),
        ],
        compiler_params=pltpu.CompilerParams(vmem_limit_bytes=48 * 1024 * 1024),
    )(blocks, table)
    conv = lax.all_to_all(conv, "ctx", split_axis=0, concat_axis=0, tiled=True)
    convolved = conv.reshape(channels_here, tokens_here).astype(f32)
    mixed = (post_gate.astype(f32) * (convolved + skip_gain[:, None] * gated_input)).astype(bf16)
    return lax.psum_scatter(
        lax.dot_general(
            out_weight, mixed, (((0,), (0,)), ((), ())), preferred_element_type=f32
        ).astype(bf16),
        "tp",
        scatter_dimension=0,
        tiled=True,
    )


MESH = pl.DeviceIdType.MESH
HALVES = 2
SUBS = 2


def fused_kernel(
    n, sig, pre, post, taps, skip, weight_hbm, table_hbm, out,
    x_send, x_recv, spec, wide, y_send, y_recv, table, weight, mixed_t, part, a_send, a_recv, c_send, c_recv,
    load_sem, xs_sem, xr_sem, ys_sem, yr_sem, as_sem, ar_sem, cs_sem, cr_sem,
):
    me = lax.axis_index("ctx")
    tp = lax.axis_index("tp")
    row, core = tp // 2, tp % 2
    partner = row * 2 + (1 - core)
    across = (1 - row) * 2 + core
    channels, width = sig.shape
    half = channels // HALVES
    ch = half // n
    feats = out.shape[0]
    sub = feats // SUBS
    order = sorted(range(1, n), key=lambda d: abs(d - n // 2))

    loads = [pltpu.make_async_copy(table_hbm, table, load_sem.at[0])]
    for f in range(4):
        loads.append(
            pltpu.make_async_copy(weight_hbm.at[:, pl.ds(f * feats, feats)], weight.at[f], load_sem.at[1 + f])
        )
    for load in loads:
        load.start()

    barrier = pltpu.get_barrier_semaphore()
    for d in range(1, n):
        pl.semaphore_signal(barrier, inc=1, device_id={"ctx": lax.rem(me + d, n)}, device_id_type=MESH)
    pl.semaphore_signal(barrier, inc=1, device_id={"tp": partner}, device_id_type=MESH)
    pl.semaphore_signal(barrier, inc=1, device_id={"tp": across}, device_id_type=MESH)

    def owned(h, peer):
        return pl.ds(pl.multiple_of(h * half + peer * ch, ch), ch)

    def gated(rows):
        return sig[rows, :].astype(f32) * pre[rows, :].astype(f32)

    x_copies = {}
    for h in range(HALVES):
        for d in order:
            rows = owned(h, lax.rem(me + d, n))
            x_send[h, d, :ch, :] = gated(rows).astype(bf16)
            x_send[h, d, ch:, :] = taps[rows, :].astype(bf16)
        if h == 0:
            pl.semaphore_wait(barrier, n + 1)
        for d in order:
            copy = pltpu.make_async_remote_copy(
                src_ref=x_send.at[h, d],
                dst_ref=x_recv.at[h, me],
                send_sem=xs_sem.at[h, d],
                recv_sem=xr_sem.at[h, d],
                device_id={"ctx": lax.rem(me + d, n)},
                device_id_type=MESH,
            )
            copy.start()
            x_copies[h, d] = copy
    for h in range(HALVES):
        rows = owned(h, me)
        x_recv[h, me, :ch, :] = gated(rows).astype(bf16)
        x_recv[h, me, ch:, :] = taps[rows, :].astype(bf16)
    loads[0].wait()

    y_copies = {}

    def mix(h):
        for d in order:
            y_copies[h, d].wait_recv()
        y_recv[owned(h, me), :] = y_send[h, me]
        step = 128
        for j in range(half // step):
            rows = pl.ds(h * half + j * step, step)
            value = post[rows, :].astype(f32) * (y_recv[rows, :].astype(f32) + skip[rows, :] * gated(rows))
            mixed_t[:, pl.ds(h * half + j * step, step)] = value.T.astype(bf16)

    for h in range(HALVES):
        for d in order:
            x_copies[h, d].wait_recv()

        def front_step(i, _):
            rows = pl.ds(pl.multiple_of(i * ROWS, ROWS), ROWS)
            front(n, rows, lambda b: x_recv[h, b, rows, :].astype(f32), spec)
            return 0

        lax.fori_loop(0, 2 * ch // ROWS, front_step, 0)
        middle(0, ch, True, spec, table, wide)
        middle(n, ch, True, spec, table, wide)

        def middle_step(k1, _):
            middle(k1, ch, False, spec, table, wide)
            return 0

        lax.fori_loop(1, n, middle_step, 0)

        def back_step(i, _):
            rows = pl.ds(pl.multiple_of(i * ROWS, ROWS), ROWS)

            def store(b, value):
                y_send[h, b, rows, :] = value.astype(bf16)

            back(n, rows, wide, store)
            return 0

        lax.fori_loop(0, ch // ROWS, back_step, 0)
        for d in order:
            peer = lax.rem(me + d, n)
            copy = pltpu.make_async_remote_copy(
                src_ref=y_send.at[h, peer],
                dst_ref=y_recv.at[owned(h, me)],
                send_sem=ys_sem.at[h, d],
                recv_sem=yr_sem.at[h, d],
                device_id={"ctx": peer},
                device_id_type=MESH,
            )
            copy.start()
            y_copies[h, d] = copy

    for load in loads[1:]:
        load.wait()
    tile = 256

    def columns(t):
        return pl.ds(pl.multiple_of(t * tile, tile), tile)

    for h in range(HALVES - 1):
        mix(h)
        for f in range(4):

            def partial_step(t, _):
                term = jnp.dot(
                    mixed_t[:, h * half : (h + 1) * half],
                    weight[f, h * half : (h + 1) * half, columns(t)],
                    preferred_element_type=f32,
                )
                part[f, :, columns(t)] = term if h == 0 else part[f, :, columns(t)] + term
                return 0

            lax.fori_loop(0, feats // tile, partial_step, 0)

    last = HALVES - 1
    mix(last)

    def project(f, t):
        return part[f, :, columns(t)] + jnp.dot(
            mixed_t[:, last * half :], weight[f, last * half :, columns(t)], preferred_element_type=f32
        )

    per_sub = sub // tile
    a_copies, c_copies = {}, {}

    def send_partner(slot, s, f):
        def step(t, _):
            a_send[slot, s, :, columns(t)] = project(f, s * per_sub + t).astype(bf16)
            return 0

        lax.fori_loop(0, per_sub, step, 0)
        copy = pltpu.make_async_remote_copy(
            src_ref=a_send.at[slot, s],
            dst_ref=a_recv.at[slot, s],
            send_sem=as_sem.at[slot, s],
            recv_sem=ar_sem.at[slot, s],
            device_id={"tp": partner},
            device_id_type=MESH,
        )
        copy.start()
        a_copies[slot, s] = copy

    for s in range(SUBS):
        send_partner(0, s, (1 - row) * 2 + (1 - core))
    for s in range(SUBS):
        a_copies[0, s].wait_recv()

        def across_step(t, _):
            total = project(across, s * per_sub + t) + a_recv[0, s, :, columns(t)].astype(f32)
            c_send[s, :, columns(t)] = total.astype(bf16)
            return 0

        lax.fori_loop(0, per_sub, across_step, 0)
        copy = pltpu.make_async_remote_copy(
            src_ref=c_send.at[s],
            dst_ref=c_recv.at[s],
            send_sem=cs_sem.at[s],
            recv_sem=cr_sem.at[s],
            device_id={"tp": across},
            device_id_type=MESH,
        )
        copy.start()
        c_copies[s] = copy
    for s in range(SUBS):
        send_partner(1, s, partner)
    for s in range(SUBS):
        a_copies[1, s].wait_recv()

        def own_step(t, _):
            where = columns(s * per_sub + t)
            part[tp, :, where] = project(tp, s * per_sub + t) + a_recv[1, s, :, columns(t)].astype(f32)
            return 0

        lax.fori_loop(0, per_sub, own_step, 0)
    for s in range(SUBS):
        c_copies[s].wait_recv()

        def out_step(t, _):
            where = columns(s * per_sub + t)
            total = part[tp, :, where] + c_recv[s, :, columns(t)].astype(f32)
            out[where, :] = total.T.astype(bf16)
            return 0

        lax.fori_loop(0, per_sub, out_step, 0)
    for group in (x_copies, y_copies, a_copies, c_copies):
        for copy in group.values():
            copy.wait_send()


def per_device_fused(signal, pre_gate, post_gate, filter_taps, skip_gain, out_weight):
    channels, width = signal.shape
    n = lax.axis_size("ctx")
    feats = out_weight.shape[1] // 4
    half = channels // HALVES
    ch = half // n
    sub = feats // SUBS
    vmem = pl.BlockSpec(memory_space=pltpu.VMEM)
    hbm = pl.BlockSpec(memory_space=pl.ANY)
    dma = pltpu.SemaphoreType.DMA
    return pl.pallas_call(
        functools.partial(fused_kernel, n),
        out_shape=jax.ShapeDtypeStruct((feats, width), bf16),
        in_specs=[vmem] * 5 + [hbm] * 2,
        out_specs=vmem,
        scratch_shapes=[
            pltpu.VMEM((HALVES, n, 2 * ch, width), bf16),
            pltpu.VMEM((HALVES, n, 2 * ch, width), bf16),
            pltpu.VMEM((n + 1, 2 * ch, 2 * width), bf16),
            pltpu.VMEM((n + 1, ch, 2 * width), f32),
            pltpu.VMEM((HALVES, n, ch, width), bf16),
            pltpu.VMEM((channels, width), bf16),
            pltpu.VMEM((n + 1, 2 * width, 2 * width), bf16),
            pltpu.VMEM((4, channels, feats), bf16),
            pltpu.VMEM((width, channels), bf16),
            pltpu.VMEM((4, width, feats), f32),
            pltpu.VMEM((2, SUBS, width, sub), bf16),
            pltpu.VMEM((2, SUBS, width, sub), bf16),
            pltpu.VMEM((SUBS, width, sub), bf16),
            pltpu.VMEM((SUBS, width, sub), bf16),
            dma((5,)),
            dma((HALVES, n)),
            dma((HALVES, n)),
            dma((HALVES, n)),
            dma((HALVES, n)),
            dma((2, SUBS)),
            dma((2, SUBS)),
            dma((SUBS,)),
            dma((SUBS,)),
        ],
        compiler_params=pltpu.CompilerParams(
            collective_id=0, has_side_effects=True, vmem_limit_bytes=56 * 1024 * 1024
        ),
    )(
        signal, pre_gate, post_gate, filter_taps, skip_gain[:, None], out_weight,
        jnp.asarray(freq_tables(n, width)),
    )


def per_device(signal, *rest):
    channels, width = signal.shape
    features = rest[-1].shape[1]
    n, tp = lax.axis_size("ctx"), lax.axis_size("tp")
    fits = n <= 8 and n % 2 == 0 and tp == 4 and width % 256 == 0
    fits = fits and channels % (HALVES * n * 16) == 0 and channels % (HALVES * 128) == 0
    fits = fits and features % (4 * SUBS * 256) == 0
    return (per_device_fused if fits else per_device_generic)(signal, *rest)


def solution(mesh):
    return jax.shard_map(
        per_device,
        mesh=mesh,
        in_specs=(
            P("tp", "ctx"),
            P("tp", "ctx"),
            P("tp", "ctx"),
            P("tp", "ctx"),
            P("tp"),
            P("tp", None),
        ),
        out_specs=P("tp", "ctx"),
        check_vma=False,
    )
```

```python
import functools
import math

import jax
import jax.numpy as jnp
import numpy as np
from jax import lax
from jax.experimental import pallas as pl
from jax.experimental.pallas import tpu as pltpu
from jax.sharding import PartitionSpec as P

f32 = jnp.float32
bf16 = jnp.bfloat16


def freq_tables(blocks, width):
    total = 2 * blocks * width
    place = np.arange(width, dtype=np.int64)
    tables = []
    for k1 in range(blocks + 1):
        angle = (place[:, None] * (k1 + 2 * blocks * place[None, :]) % total) * (2.0 * math.pi / total)
        c, s = np.cos(angle), np.sin(angle)
        tables.append(np.block([[c, -s], [s, c]]))
    return np.stack(tables).astype(jnp.bfloat16)


def weighted(terms):
    total = None
    for coef, part in terms:
        if abs(coef) < 1e-12:
            continue
        value = part if coef == 1.0 else (-part if coef == -1.0 else part * coef)
        total = value if total is None else total + value
    return total


def unit(fn, b, k1, n):
    value = fn(math.pi * (b * k1 % (2 * n)) / n)
    return float(round(value)) if abs(value - round(value)) < 1e-12 else value


def front(n, rows, load, spec):
    width = spec.shape[-1] // 2
    x = [load(b) for b in range(n)]
    even, odd = range(0, n, 2), range(1, n, 2)
    for k1 in range(n // 2 + 1):
        ce = weighted([(unit(math.cos, b, k1, n), x[b]) for b in even])
        co = weighted([(unit(math.cos, b, k1, n), x[b]) for b in odd])
        se = weighted([(unit(math.sin, b, k1, n), x[b]) for b in even])
        so = weighted([(unit(math.sin, b, k1, n), x[b]) for b in odd])
        k2 = n - k1
        if k1 == k2:
            spec[k1, rows, :width] = ce.astype(bf16)
            spec[k1, rows, width:] = (-so).astype(bf16)
            continue
        spec[k1, rows, :width] = (ce + co).astype(bf16)
        spec[k2, rows, :width] = (ce - co).astype(bf16)
        if k1:
            spec[k1, rows, width:] = (-(se + so)).astype(bf16)
            spec[k2, rows, width:] = (se - so).astype(bf16)


def middle(k1, channels, real_only, spec, table, wide):
    width = table.shape[-1] // 2
    depth = width if real_only else 2 * width
    full = jnp.dot(spec[k1, :, :depth], table[k1, :depth, :], preferred_element_type=f32)
    ur, ui = full[:channels, :width], full[:channels, width:]
    hr, hi = full[channels:, :width], full[channels:, width:]
    prod = jnp.concatenate([ur * hr - ui * hi, ur * hi + ui * hr], axis=1).astype(bf16)
    wide[k1, :, :depth] = lax.dot_general(
        prod, table[k1, :depth, :], (((1,), (1,)), ((), ())), preferred_element_type=f32
    )


def back(n, rows, wide, store):
    width = wide.shape[-1] // 2
    scale = 1.0 / (2 * n * width)
    re = [wide[k, rows, :width] for k in range(n + 1)]
    im = [None if k in (0, n) else wide[k, rows, width:] for k in range(n + 1)]
    for parity in (0, 1):
        sign = 1.0 if parity == 0 else -1.0
        reals, imags = [], []
        for k in range(n // 2):
            reals.append(re[k] + re[n - k] if parity == 0 else re[k] - re[n - k])
            imags.append(None if k == 0 else (im[k] - im[n - k] if parity == 0 else im[k] + im[n - k]))
        for b in range(parity, n, 2):
            terms = []
            for k in range(n // 2):
                weight = scale if k == 0 else 2.0 * scale
                terms.append((weight * unit(math.cos, b, k, n), reals[k]))
                if k:
                    terms.append((-weight * unit(math.sin, b, k, n), imags[k]))
            if parity == 0:
                terms.append((2.0 * scale * unit(math.cos, b, n // 2, n), re[n // 2]))
            else:
                terms.append((-2.0 * scale * unit(math.sin, b, n // 2, n), im[n // 2]))
            terms = [(c if abs(c) > 1e-9 * scale else 0.0, v) for c, v in terms]
            store(b, weighted([(c / scale, v) for c, v in terms]) * scale)


ROWS = 16


def conv_kernel(n, x_ref, table, y_ref, spec, wide):
    channels = y_ref.shape[1]

    def front_step(i, _):
        rows = pl.ds(pl.multiple_of(i * ROWS, ROWS), ROWS)
        front(n, rows, lambda b: x_ref[b, rows, :].astype(f32), spec)
        return 0

    lax.fori_loop(0, 2 * channels // ROWS, front_step, 0)
    middle(0, channels, True, spec, table, wide)
    middle(n, channels, True, spec, table, wide)

    def middle_step(k1, _):
        middle(k1, channels, False, spec, table, wide)
        return 0

    lax.fori_loop(1, n, middle_step, 0)

    height = min(ROWS, channels)

    def back_step(i, _):
        rows = pl.ds(pl.multiple_of(i * height, height), height)

        def store(b, value):
            y_ref[b, rows, :] = value.astype(bf16)

        back(n, rows, wide, store)
        return 0

    lax.fori_loop(0, channels // height, back_step, 0)


def per_device_generic(signal, pre_gate, post_gate, filter_taps, skip_gain, out_weight):
    channels_here, tokens_here = signal.shape
    n = lax.axis_size("ctx")
    mine = channels_here // n
    gated_input = signal.astype(f32) * pre_gate.astype(f32)
    stacked = jnp.stack([gated_input.astype(bf16), filter_taps.astype(bf16)])
    stacked = stacked.reshape(2, n, mine, tokens_here).transpose(1, 0, 2, 3).reshape(n, 2 * mine, tokens_here)
    blocks = lax.all_to_all(stacked, "ctx", split_axis=0, concat_axis=0, tiled=True)
    table = jnp.asarray(freq_tables(n, tokens_here))
    conv = pl.pallas_call(
        functools.partial(conv_kernel, n),
        out_shape=jax.ShapeDtypeStruct((n, mine, tokens_here), bf16),
        in_specs=[pl.BlockSpec(memory_space=pltpu.VMEM)] * 2,
        out_specs=pl.BlockSpec(memory_space=pltpu.VMEM),
        scratch_shapes=[
            pltpu.VMEM((n + 1, 2 * mine, 2 * tokens_here), bf16),
            pltpu.VMEM((n + 1, mine, 2 * tokens_here), f32),
        ],
        compiler_params=pltpu.CompilerParams(vmem_limit_bytes=48 * 1024 * 1024),
    )(blocks, table)
    conv = lax.all_to_all(conv, "ctx", split_axis=0, concat_axis=0, tiled=True)
    convolved = conv.reshape(channels_here, tokens_here).astype(f32)
    mixed = (post_gate.astype(f32) * (convolved + skip_gain[:, None] * gated_input)).astype(bf16)
    return lax.psum_scatter(
        lax.dot_general(
            out_weight, mixed, (((0,), (0,)), ((), ())), preferred_element_type=f32
        ).astype(bf16),
        "tp",
        scatter_dimension=0,
        tiled=True,
    )


MESH = pl.DeviceIdType.MESH
HALVES = 2
SUBS = 2


def fused_kernel(
    n, sig, pre, post, taps, skip, weight_hbm, table_hbm, out,
    x_send, x_recv, spec, wide, y_send, y_recv, table, weight, mixed_t, part, a_send, a_recv, c_send, c_recv,
    load_sem, xs_sem, xr_sem, ys_sem, yr_sem, as_sem, ar_sem, cs_sem, cr_sem,
):
    me = lax.axis_index("ctx")
    tp = lax.axis_index("tp")
    row, core = tp // 2, tp % 2
    partner = row * 2 + (1 - core)
    across = (1 - row) * 2 + core
    channels, width = sig.shape
    half = channels // HALVES
    ch = half // n
    feats = out.shape[0]
    order = sorted(range(1, n), key=lambda m: -(m // 2))
    span = width // SUBS

    def peer_of(mask):
        peer, bit = me, 1
        while bit < n:
            if mask // bit % 2:
                peer = peer + bit * (1 - 2 * ((me // bit) % 2))
            bit *= 2
        return peer


    loads = [pltpu.make_async_copy(table_hbm, table, load_sem.at[0])]
    for f in range(4):
        loads.append(
            pltpu.make_async_copy(weight_hbm.at[:, pl.ds(f * feats, feats)], weight.at[f], load_sem.at[1 + f])
        )
    for load in loads:
        load.start()

    barrier = pltpu.get_barrier_semaphore()
    for d in range(1, n):
        pl.semaphore_signal(barrier, inc=1, device_id={"ctx": peer_of(d)}, device_id_type=MESH)
    pl.semaphore_signal(barrier, inc=1, device_id={"tp": partner}, device_id_type=MESH)
    pl.semaphore_signal(barrier, inc=1, device_id={"tp": across}, device_id_type=MESH)

    def owned(h, peer):
        return pl.ds(pl.multiple_of(h * half + peer * ch, ch), ch)

    def gated(rows):
        return sig[rows, :].astype(f32) * pre[rows, :].astype(f32)

    x_copies = {}
    for h in range(HALVES):
        for d in order:
            rows = owned(h, peer_of(d))
            x_send[h, d, :ch, :] = gated(rows).astype(bf16)
            x_send[h, d, ch:, :] = taps[rows, :].astype(bf16)
        if h == 0:
            pl.semaphore_wait(barrier, n + 1)
        for d in order:
            copy = pltpu.make_async_remote_copy(
                src_ref=x_send.at[h, d],
                dst_ref=x_recv.at[h, me],
                send_sem=xs_sem.at[h, d],
                recv_sem=xr_sem.at[h, d],
                device_id={"ctx": peer_of(d)},
                device_id_type=MESH,
            )
            copy.start()
            x_copies[h, d] = copy
    for h in range(HALVES):
        rows = owned(h, me)
        x_recv[h, me, :ch, :] = gated(rows).astype(bf16)
        x_recv[h, me, ch:, :] = taps[rows, :].astype(bf16)
    loads[0].wait()

    y_copies = {}
    skip_t = skip[...].T

    def mix(h, t):
        for d in order:
            y_copies[h, t, d].wait_recv()
        y_recv[t, owned(h, me), :] = y_send[h, t, me]
        step = 128
        tokens = pl.ds(t * span, span)
        for j in range(h * half // step, (h + 1) * half // step):
            rows = pl.ds(j * step, step)
            gate_in = sig[rows, tokens].astype(f32) * pre[rows, tokens].astype(f32)
            conv = y_recv[t, rows, :].astype(f32)
            value = post[rows, tokens].astype(f32) * (conv + skip_t[:, j : j + 1] * gate_in)
            mixed_t[tokens, rows] = value.T.astype(bf16)

    def send_back(h, t):
        for d in order:
            peer = peer_of(d)
            copy = pltpu.make_async_remote_copy(
                src_ref=y_send.at[h, t, peer],
                dst_ref=y_recv.at[t, owned(h, me)],
                send_sem=ys_sem.at[h, t, d],
                recv_sem=yr_sem.at[h, t, d],
                device_id={"ctx": peer},
                device_id_type=MESH,
            )
            copy.start()
            y_copies[h, t, d] = copy

    for h in range(HALVES):
        for d in order:
            x_copies[h, d].wait_recv()
        if h == HALVES - 1:
            for earlier in range(h):
                for t in range(SUBS):
                    send_back(earlier, t)

        def front_step(i, _):
            rows = pl.ds(pl.multiple_of(i * ROWS, ROWS), ROWS)
            front(n, rows, lambda b: x_recv[h, b, rows, :].astype(f32), spec)
            return 0

        lax.fori_loop(0, 2 * ch // ROWS, front_step, 0)
        middle(0, ch, True, spec, table, wide)
        middle(n, ch, True, spec, table, wide)

        def middle_step(k1, _):
            middle(k1, ch, False, spec, table, wide)
            return 0

        lax.fori_loop(1, n, middle_step, 0)

        def back_step(i, _):
            rows = pl.ds(pl.multiple_of(i * ROWS, ROWS), ROWS)

            def store(b, value):
                for t in range(SUBS):
                    y_send[h, t, b, rows, :] = value[:, t * span : (t + 1) * span].astype(bf16)

            back(n, rows, wide, store)
            return 0

        lax.fori_loop(0, ch // ROWS, back_step, 0)
    for t in range(SUBS):
        send_back(HALVES - 1, t)

    for load in loads[1:]:
        load.wait()
    tile = 256

    def columns(t):
        return pl.ds(pl.multiple_of(t * tile, tile), tile)

    for h in range(HALVES - 1):
        for t in range(SUBS):
            mix(h, t)
        for f in range(4):

            def partial_step(c, _):
                term = jnp.dot(
                    mixed_t[:, h * half : (h + 1) * half],
                    weight[f, h * half : (h + 1) * half, columns(c)],
                    preferred_element_type=f32,
                )
                part[f, :, columns(c)] = term if h == 0 else part[f, :, columns(c)] + term
                return 0

            lax.fori_loop(0, feats // tile, partial_step, 0)

    last = HALVES - 1
    tiles = feats // tile

    def project(f, t, c):
        tokens = pl.ds(t * span, span)
        return part[f, tokens, columns(c)] + jnp.dot(
            mixed_t[tokens, last * half :], weight[f, last * half :, columns(c)], preferred_element_type=f32
        )

    a_copies, c_copies = {}, {}

    def send_partner(slot, t, f):
        def step(c, _):
            a_send[slot, t, :, columns(c)] = project(f, t, c).astype(bf16)
            return 0

        lax.fori_loop(0, tiles, step, 0)
        copy = pltpu.make_async_remote_copy(
            src_ref=a_send.at[slot, t],
            dst_ref=a_recv.at[slot, t],
            send_sem=as_sem.at[slot, t],
            recv_sem=ar_sem.at[slot, t],
            device_id={"tp": partner},
            device_id_type=MESH,
        )
        copy.start()
        a_copies[slot, t] = copy

    for t in range(SUBS):
        tokens = pl.ds(t * span, span)
        mix(last, t)
        send_partner(0, t, (1 - row) * 2 + (1 - core))

        def ahead_step(c, _):
            part[across, tokens, columns(c)] = project(across, t, c)
            return 0

        lax.fori_loop(0, tiles, ahead_step, 0)
        a_copies[0, t].wait_recv()

        def across_step(c, _):
            total = part[across, tokens, columns(c)] + a_recv[0, t, :, columns(c)].astype(f32)
            c_send[t, :, columns(c)] = total.astype(bf16)
            return 0

        lax.fori_loop(0, tiles, across_step, 0)
        copy = pltpu.make_async_remote_copy(
            src_ref=c_send.at[t],
            dst_ref=c_recv.at[t],
            send_sem=cs_sem.at[t],
            recv_sem=cr_sem.at[t],
            device_id={"tp": across},
            device_id_type=MESH,
        )
        copy.start()
        c_copies[t] = copy
    for t in range(SUBS):
        send_partner(1, t, partner)
    for t in range(SUBS):
        tokens = pl.ds(t * span, span)
        a_copies[1, t].wait_recv()

        def own_step(c, _):
            part[tp, tokens, columns(c)] = project(tp, t, c) + a_recv[1, t, :, columns(c)].astype(f32)
            return 0

        lax.fori_loop(0, tiles, own_step, 0)
    for t in range(SUBS):
        tokens = pl.ds(t * span, span)
        c_copies[t].wait_recv()

        def out_step(c, _):
            total = part[tp, tokens, columns(c)] + c_recv[t, :, columns(c)].astype(f32)
            out[columns(c), tokens] = total.T.astype(bf16)
            return 0

        lax.fori_loop(0, tiles, out_step, 0)
    for group in (x_copies, y_copies, a_copies, c_copies):
        for copy in group.values():
            copy.wait_send()


def per_device_fused(signal, pre_gate, post_gate, filter_taps, skip_gain, out_weight):
    channels, width = signal.shape
    n = lax.axis_size("ctx")
    feats = out_weight.shape[1] // 4
    half = channels // HALVES
    ch = half // n
    span = width // SUBS
    vmem = pl.BlockSpec(memory_space=pltpu.VMEM)
    hbm = pl.BlockSpec(memory_space=pl.ANY)
    dma = pltpu.SemaphoreType.DMA
    return pl.pallas_call(
        functools.partial(fused_kernel, n),
        out_shape=jax.ShapeDtypeStruct((feats, width), bf16),
        in_specs=[vmem] * 5 + [hbm] * 2,
        out_specs=vmem,
        scratch_shapes=[
            pltpu.VMEM((HALVES, n, 2 * ch, width), bf16),
            pltpu.VMEM((HALVES, n, 2 * ch, width), bf16),
            pltpu.VMEM((n + 1, 2 * ch, 2 * width), bf16),
            pltpu.VMEM((n + 1, ch, 2 * width), f32),
            pltpu.VMEM((HALVES, SUBS, n, ch, span), bf16),
            pltpu.VMEM((SUBS, channels, span), bf16),
            pltpu.VMEM((n + 1, 2 * width, 2 * width), bf16),
            pltpu.VMEM((4, channels, feats), bf16),
            pltpu.VMEM((width, channels), bf16),
            pltpu.VMEM((4, width, feats), f32),
            pltpu.VMEM((2, SUBS, span, feats), bf16),
            pltpu.VMEM((2, SUBS, span, feats), bf16),
            pltpu.VMEM((SUBS, span, feats), bf16),
            pltpu.VMEM((SUBS, span, feats), bf16),
            dma((5,)),
            dma((HALVES, n)),
            dma((HALVES, n)),
            dma((HALVES, SUBS, n)),
            dma((HALVES, SUBS, n)),
            dma((2, SUBS)),
            dma((2, SUBS)),
            dma((SUBS,)),
            dma((SUBS,)),
        ],
        compiler_params=pltpu.CompilerParams(
            collective_id=0, has_side_effects=True, vmem_limit_bytes=56 * 1024 * 1024
        ),
    )(
        signal, pre_gate, post_gate, filter_taps, skip_gain.reshape(channels // 128, 128), out_weight,
        jnp.asarray(freq_tables(n, width)),
    )


def per_device(signal, *rest):
    channels, width = signal.shape
    features = rest[-1].shape[1]
    n, tp = lax.axis_size("ctx"), lax.axis_size("tp")
    fits = n in (2, 4, 8) and tp == 4 and width % 256 == 0
    fits = fits and channels % (HALVES * n * 16) == 0 and channels % (HALVES * 128) == 0
    fits = fits and features % (4 * 256) == 0
    return (per_device_fused if fits else per_device_generic)(signal, *rest)


def solution(mesh):
    return jax.shard_map(
        per_device,
        mesh=mesh,
        in_specs=(
            P("tp", "ctx"),
            P("tp", "ctx"),
            P("tp", "ctx"),
            P("tp", "ctx"),
            P("tp"),
            P("tp", None),
        ),
        out_specs=P("tp", "ctx"),
        check_vma=False,
    )
```

```python
import functools
import math

import jax
import jax.numpy as jnp
import numpy as np
from jax import lax
from jax.experimental import pallas as pl
from jax.experimental.pallas import tpu as pltpu
from jax.sharding import PartitionSpec as P

f32 = jnp.float32
bf16 = jnp.bfloat16


def freq_tables(blocks, width):
    total = 2 * blocks * width
    place = np.arange(width, dtype=np.int64)
    tables = []
    for k1 in range(blocks + 1):
        angle = (place[:, None] * (k1 + 2 * blocks * place[None, :]) % total) * (2.0 * math.pi / total)
        c, s = np.cos(angle), np.sin(angle)
        tables.append(np.block([[c, -s], [s, c]]))
    return np.stack(tables).astype(jnp.bfloat16)


def weighted(terms):
    total = None
    for coef, part in terms:
        if abs(coef) < 1e-12:
            continue
        value = part if coef == 1.0 else (-part if coef == -1.0 else part * coef)
        total = value if total is None else total + value
    return total


def unit(fn, b, k1, n):
    value = fn(math.pi * (b * k1 % (2 * n)) / n)
    return float(round(value)) if abs(value - round(value)) < 1e-12 else value


def front(n, rows, load, spec):
    width = spec.shape[-1] // 2
    x = [load(b) for b in range(n)]
    even, odd = range(0, n, 2), range(1, n, 2)
    for k1 in range(n // 2 + 1):
        ce = weighted([(unit(math.cos, b, k1, n), x[b]) for b in even])
        co = weighted([(unit(math.cos, b, k1, n), x[b]) for b in odd])
        se = weighted([(unit(math.sin, b, k1, n), x[b]) for b in even])
        so = weighted([(unit(math.sin, b, k1, n), x[b]) for b in odd])
        k2 = n - k1
        if k1 == k2:
            spec[k1, rows, :width] = ce.astype(bf16)
            spec[k1, rows, width:] = (-so).astype(bf16)
            continue
        spec[k1, rows, :width] = (ce + co).astype(bf16)
        spec[k2, rows, :width] = (ce - co).astype(bf16)
        if k1:
            spec[k1, rows, width:] = (-(se + so)).astype(bf16)
            spec[k2, rows, width:] = (se - so).astype(bf16)


def middle(k1, channels, real_only, spec, table, wide):
    width = table.shape[-1] // 2
    depth = width if real_only else 2 * width
    full = jnp.dot(spec[k1, : 2 * channels, :depth], table[k1, :depth, :], preferred_element_type=f32)
    ur, ui = full[:channels, :width], full[:channels, width:]
    hr, hi = full[channels:, :width], full[channels:, width:]
    prod = jnp.concatenate([ur * hr - ui * hi, ur * hi + ui * hr], axis=1).astype(bf16)
    wide[k1, :channels, :depth] = lax.dot_general(
        prod, table[k1, :depth, :], (((1,), (1,)), ((), ())), preferred_element_type=f32
    )


def back(n, rows, wide, store):
    width = wide.shape[-1] // 2
    scale = 1.0 / (2 * n * width)
    re = [wide[k, rows, :width] for k in range(n + 1)]
    im = [None if k in (0, n) else wide[k, rows, width:] for k in range(n + 1)]
    for parity in (0, 1):
        sign = 1.0 if parity == 0 else -1.0
        reals, imags = [], []
        for k in range(n // 2):
            reals.append(re[k] + re[n - k] if parity == 0 else re[k] - re[n - k])
            imags.append(None if k == 0 else (im[k] - im[n - k] if parity == 0 else im[k] + im[n - k]))
        for b in range(parity, n, 2):
            terms = []
            for k in range(n // 2):
                weight = scale if k == 0 else 2.0 * scale
                terms.append((weight * unit(math.cos, b, k, n), reals[k]))
                if k:
                    terms.append((-weight * unit(math.sin, b, k, n), imags[k]))
            if parity == 0:
                terms.append((2.0 * scale * unit(math.cos, b, n // 2, n), re[n // 2]))
            else:
                terms.append((-2.0 * scale * unit(math.sin, b, n // 2, n), im[n // 2]))
            terms = [(c if abs(c) > 1e-9 * scale else 0.0, v) for c, v in terms]
            store(b, weighted([(c / scale, v) for c, v in terms]) * scale)


ROWS = 16


def conv_kernel(n, x_ref, table, y_ref, spec, wide):
    channels = y_ref.shape[1]

    def front_step(i, _):
        rows = pl.ds(pl.multiple_of(i * ROWS, ROWS), ROWS)
        front(n, rows, lambda b: x_ref[b, rows, :].astype(f32), spec)
        return 0

    lax.fori_loop(0, 2 * channels // ROWS, front_step, 0)
    middle(0, channels, True, spec, table, wide)
    middle(n, channels, True, spec, table, wide)

    def middle_step(k1, _):
        middle(k1, channels, False, spec, table, wide)
        return 0

    lax.fori_loop(1, n, middle_step, 0)

    height = min(ROWS, channels)

    def back_step(i, _):
        rows = pl.ds(pl.multiple_of(i * height, height), height)

        def store(b, value):
            y_ref[b, rows, :] = value.astype(bf16)

        back(n, rows, wide, store)
        return 0

    lax.fori_loop(0, channels // height, back_step, 0)


def per_device_generic(signal, pre_gate, post_gate, filter_taps, skip_gain, out_weight):
    channels_here, tokens_here = signal.shape
    n = lax.axis_size("ctx")
    mine = channels_here // n
    gated_input = signal.astype(f32) * pre_gate.astype(f32)
    stacked = jnp.stack([gated_input.astype(bf16), filter_taps.astype(bf16)])
    stacked = stacked.reshape(2, n, mine, tokens_here).transpose(1, 0, 2, 3).reshape(n, 2 * mine, tokens_here)
    blocks = lax.all_to_all(stacked, "ctx", split_axis=0, concat_axis=0, tiled=True)
    table = jnp.asarray(freq_tables(n, tokens_here))
    conv = pl.pallas_call(
        functools.partial(conv_kernel, n),
        out_shape=jax.ShapeDtypeStruct((n, mine, tokens_here), bf16),
        in_specs=[pl.BlockSpec(memory_space=pltpu.VMEM)] * 2,
        out_specs=pl.BlockSpec(memory_space=pltpu.VMEM),
        scratch_shapes=[
            pltpu.VMEM((n + 1, 2 * mine, 2 * tokens_here), bf16),
            pltpu.VMEM((n + 1, mine, 2 * tokens_here), f32),
        ],
        compiler_params=pltpu.CompilerParams(vmem_limit_bytes=48 * 1024 * 1024),
    )(blocks, table)
    conv = lax.all_to_all(conv, "ctx", split_axis=0, concat_axis=0, tiled=True)
    convolved = conv.reshape(channels_here, tokens_here).astype(f32)
    mixed = (post_gate.astype(f32) * (convolved + skip_gain[:, None] * gated_input)).astype(bf16)
    return lax.psum_scatter(
        lax.dot_general(
            out_weight, mixed, (((0,), (0,)), ((), ())), preferred_element_type=f32
        ).astype(bf16),
        "tp",
        scatter_dimension=0,
        tiled=True,
    )


MESH = pl.DeviceIdType.MESH
CHUNKS = 2
SUBS = 2


def chunk_sizes(mine):
    return (mine - mine // 4, mine // 4)


def fused_kernel(
    n, sig, pre, post, taps, skip, weight_hbm, table_hbm, out,
    x_send, x_recv, spec, wide, y_send, y_recv, table, weight, mixed_t, part, a_send, a_recv, c_send, c_recv,
    load_sem, xs_sem, xr_sem, ys_sem, yr_sem, as_sem, ar_sem, cs_sem, cr_sem,
):
    me = lax.axis_index("ctx")
    tp = lax.axis_index("tp")
    row, core = tp // 2, tp % 2
    partner = row * 2 + (1 - core)
    across = (1 - row) * 2 + core
    channels, width = sig.shape
    sizes = chunk_sizes(channels // n)
    offsets = (0, sizes[0])
    feats = out.shape[0]
    order = sorted(range(1, n), key=lambda m: -(m // 2))
    span = width // SUBS

    def peer_of(mask):
        peer, bit = me, 1
        while bit < n:
            if mask // bit % 2:
                peer = peer + bit * (1 - 2 * ((me // bit) % 2))
            bit *= 2
        return peer


    loads = [pltpu.make_async_copy(table_hbm, table, load_sem.at[0])]
    for f in range(4):
        loads.append(
            pltpu.make_async_copy(weight_hbm.at[:, pl.ds(f * feats, feats)], weight.at[f], load_sem.at[1 + f])
        )
    for load in loads:
        load.start()

    barrier = pltpu.get_barrier_semaphore()
    for d in range(1, n):
        pl.semaphore_signal(barrier, inc=1, device_id={"ctx": peer_of(d)}, device_id_type=MESH)
    pl.semaphore_signal(barrier, inc=1, device_id={"tp": partner}, device_id_type=MESH)
    pl.semaphore_signal(barrier, inc=1, device_id={"tp": across}, device_id_type=MESH)

    def owned(h, peer):
        return pl.ds(pl.multiple_of(n * offsets[h] + peer * sizes[h], 16), sizes[h])

    def pair(h):
        return pl.ds(2 * offsets[h], 2 * sizes[h])

    def gated(rows):
        return sig[rows, :].astype(f32) * pre[rows, :].astype(f32)

    def fill(ref, slot, h, peer):
        rows = owned(h, peer)
        middle_row = 2 * offsets[h] + sizes[h]
        ref[slot, pl.ds(2 * offsets[h], sizes[h]), :] = gated(rows).astype(bf16)
        ref[slot, pl.ds(middle_row, sizes[h]), :] = taps[rows, :].astype(bf16)

    x_copies = {}
    for h in range(CHUNKS):
        for d in order:
            fill(x_send, d, h, peer_of(d))
        if h == 0:
            pl.semaphore_wait(barrier, n + 1)
        for d in order:
            copy = pltpu.make_async_remote_copy(
                src_ref=x_send.at[d, pair(h)],
                dst_ref=x_recv.at[me, pair(h)],
                send_sem=xs_sem.at[h, d],
                recv_sem=xr_sem.at[h, d],
                device_id={"ctx": peer_of(d)},
                device_id_type=MESH,
            )
            copy.start()
            x_copies[h, d] = copy
    for h in range(CHUNKS):
        fill(x_recv, me, h, me)
    loads[0].wait()

    y_copies = {}
    skip_t = skip[...].T

    def mix(h, t):
        for d in order:
            y_copies[h, t, d].wait_recv()
        y_recv[t, owned(h, me), :] = y_send[t, me, pl.ds(offsets[h], sizes[h])]
        step = 128
        tokens = pl.ds(t * span, span)
        first = n * offsets[h] // step
        for j in range(first, first + n * sizes[h] // step):
            rows = pl.ds(j * step, step)
            gate_in = sig[rows, tokens].astype(f32) * pre[rows, tokens].astype(f32)
            conv = y_recv[t, rows, :].astype(f32)
            value = post[rows, tokens].astype(f32) * (conv + skip_t[:, j : j + 1] * gate_in)
            mixed_t[tokens, rows] = value.T.astype(bf16)

    def send_back(h, t):
        for d in order:
            peer = peer_of(d)
            copy = pltpu.make_async_remote_copy(
                src_ref=y_send.at[t, peer, pl.ds(offsets[h], sizes[h])],
                dst_ref=y_recv.at[t, owned(h, me)],
                send_sem=ys_sem.at[h, t, d],
                recv_sem=yr_sem.at[h, t, d],
                device_id={"ctx": peer},
                device_id_type=MESH,
            )
            copy.start()
            y_copies[h, t, d] = copy

    for h in range(CHUNKS):
        for d in order:
            x_copies[h, d].wait_recv()
        if h == 1:
            send_back(0, 0)
        size = sizes[h]

        def front_step(i, _):
            rows = pl.ds(pl.multiple_of(i * ROWS, ROWS), ROWS)
            source = pl.ds(pl.multiple_of(2 * offsets[h] + i * ROWS, ROWS), ROWS)
            front(n, rows, lambda b: x_recv[b, source, :].astype(f32), spec)
            return 0

        lax.fori_loop(0, 2 * size // ROWS, front_step, 0)
        middle(0, size, True, spec, table, wide)
        middle(n, size, True, spec, table, wide)

        def middle_step(k1, _):
            middle(k1, size, False, spec, table, wide)
            return 0

        lax.fori_loop(1, n, middle_step, 0)

        def back_step(i, _):
            rows = pl.ds(pl.multiple_of(i * ROWS, ROWS), ROWS)
            target = pl.ds(pl.multiple_of(offsets[h] + i * ROWS, ROWS), ROWS)

            def store(b, value):
                for t in range(SUBS):
                    y_send[t, b, target, :] = value[:, t * span : (t + 1) * span].astype(bf16)

            back(n, rows, wide, store)
            return 0

        lax.fori_loop(0, size // ROWS, back_step, 0)
    send_back(1, 0)
    for t in range(1, SUBS):
        send_back(0, t)
        send_back(1, t)

    for load in loads[1:]:
        load.wait()
    tile = 256
    tiles = feats // tile
    head = n * sizes[0]

    def columns(c):
        return pl.ds(pl.multiple_of(c * tile, tile), tile)

    def project(f, t, c, lo, hi):
        return jnp.dot(
            mixed_t[t * span : (t + 1) * span, lo:hi], weight[f, lo:hi, columns(c)], preferred_element_type=f32
        )

    def each_tile(body):
        def step(c, _):
            body(c)
            return 0

        lax.fori_loop(0, tiles, step, 0)

    def to_partner(slot, t):
        copy = pltpu.make_async_remote_copy(
            src_ref=a_send.at[slot, t],
            dst_ref=a_recv.at[slot, t],
            send_sem=as_sem.at[slot, t],
            recv_sem=ar_sem.at[slot, t],
            device_id={"tp": partner},
            device_id_type=MESH,
        )
        copy.start()
        return copy

    a_copies, c_copies = {}, {}
    far = (1 - row) * 2 + (1 - core)
    for t in range(SUBS):
        tokens = pl.ds(t * span, span)
        mix(0, t)

        def early(c):
            part[far, tokens, columns(c)] = project(far, t, c, 0, head)
            part[across, tokens, columns(c)] = project(across, t, c, 0, head)

        each_tile(early)
        mix(1, t)

        def far_rest(c):
            total = part[far, tokens, columns(c)] + project(far, t, c, head, channels)
            a_send[0, t, :, columns(c)] = total.astype(bf16)

        each_tile(far_rest)
        a_copies[0, t] = to_partner(0, t)

        def across_rest(c):
            part[across, tokens, columns(c)] += project(across, t, c, head, channels)

        each_tile(across_rest)
        a_copies[0, t].wait_recv()

        def across_sum(c):
            total = part[across, tokens, columns(c)] + a_recv[0, t, :, columns(c)].astype(f32)
            c_send[t, :, columns(c)] = total.astype(bf16)

        each_tile(across_sum)
        copy = pltpu.make_async_remote_copy(
            src_ref=c_send.at[t],
            dst_ref=c_recv.at[t],
            send_sem=cs_sem.at[t],
            recv_sem=cr_sem.at[t],
            device_id={"tp": across},
            device_id_type=MESH,
        )
        copy.start()
        c_copies[t] = copy

        def partner_all(c):
            a_send[1, t, :, columns(c)] = project(partner, t, c, 0, channels).astype(bf16)

        each_tile(partner_all)
        a_copies[1, t] = to_partner(1, t)

        def own_all(c):
            part[tp, tokens, columns(c)] = project(tp, t, c, 0, channels)

        each_tile(own_all)
    for t in range(SUBS):
        tokens = pl.ds(t * span, span)
        a_copies[1, t].wait_recv()
        c_copies[t].wait_recv()

        def finish(c):
            total = part[tp, tokens, columns(c)] + a_recv[1, t, :, columns(c)].astype(f32)
            total = total + c_recv[t, :, columns(c)].astype(f32)
            out[columns(c), tokens] = total.T.astype(bf16)

        each_tile(finish)
    for group in (x_copies, y_copies, a_copies, c_copies):
        for copy in group.values():
            copy.wait_send()


def per_device_fused(signal, pre_gate, post_gate, filter_taps, skip_gain, out_weight):
    channels, width = signal.shape
    n = lax.axis_size("ctx")
    feats = out_weight.shape[1] // 4
    mine = channels // n
    most = max(chunk_sizes(mine))
    span = width // SUBS
    vmem = pl.BlockSpec(memory_space=pltpu.VMEM)
    hbm = pl.BlockSpec(memory_space=pl.ANY)
    dma = pltpu.SemaphoreType.DMA
    return pl.pallas_call(
        functools.partial(fused_kernel, n),
        out_shape=jax.ShapeDtypeStruct((feats, width), bf16),
        in_specs=[vmem] * 5 + [hbm] * 2,
        out_specs=vmem,
        scratch_shapes=[
            pltpu.VMEM((n, 2 * mine, width), bf16),
            pltpu.VMEM((n, 2 * mine, width), bf16),
            pltpu.VMEM((n + 1, 2 * most, 2 * width), bf16),
            pltpu.VMEM((n + 1, most, 2 * width), f32),
            pltpu.VMEM((SUBS, n, mine, span), bf16),
            pltpu.VMEM((SUBS, channels, span), bf16),
            pltpu.VMEM((n + 1, 2 * width, 2 * width), bf16),
            pltpu.VMEM((4, channels, feats), bf16),
            pltpu.VMEM((width, channels), bf16),
            pltpu.VMEM((4, width, feats), f32),
            pltpu.VMEM((2, SUBS, span, feats), bf16),
            pltpu.VMEM((2, SUBS, span, feats), bf16),
            pltpu.VMEM((SUBS, span, feats), bf16),
            pltpu.VMEM((SUBS, span, feats), bf16),
            dma((5,)),
            dma((CHUNKS, n)),
            dma((CHUNKS, n)),
            dma((CHUNKS, SUBS, n)),
            dma((CHUNKS, SUBS, n)),
            dma((2, SUBS)),
            dma((2, SUBS)),
            dma((SUBS,)),
            dma((SUBS,)),
        ],
        compiler_params=pltpu.CompilerParams(
            collective_id=0, has_side_effects=True, vmem_limit_bytes=56 * 1024 * 1024
        ),
    )(
        signal, pre_gate, post_gate, filter_taps, skip_gain.reshape(channels // 128, 128), out_weight,
        jnp.asarray(freq_tables(n, width)),
    )


def per_device(signal, *rest):
    channels, width = signal.shape
    features = rest[-1].shape[1]
    n, tp = lax.axis_size("ctx"), lax.axis_size("tp")
    fits = n in (2, 4, 8) and tp == 4 and width % 256 == 0
    fits = fits and channels % (4 * n * 16) == 0 and channels % (4 * 128) == 0
    fits = fits and features % (4 * 256) == 0
    return (per_device_fused if fits else per_device_generic)(signal, *rest)


def solution(mesh):
    return jax.shard_map(
        per_device,
        mesh=mesh,
        in_specs=(
            P("tp", "ctx"),
            P("tp", "ctx"),
            P("tp", "ctx"),
            P("tp", "ctx"),
            P("tp"),
            P("tp", None),
        ),
        out_specs=P("tp", "ctx"),
        check_vma=False,
    )
```

```python
import functools
import math

import jax
import jax.numpy as jnp
import numpy as np
from jax import lax
from jax.experimental import pallas as pl
from jax.experimental.pallas import tpu as pltpu
from jax.sharding import PartitionSpec as P

f32 = jnp.float32
bf16 = jnp.bfloat16


def freq_tables(blocks, width):
    total = 2 * blocks * width
    place = np.arange(width, dtype=np.int64)
    tables = []
    for k1 in range(blocks + 1):
        angle = (place[:, None] * (k1 + 2 * blocks * place[None, :]) % total) * (2.0 * math.pi / total)
        c, s = np.cos(angle), np.sin(angle)
        tables.append(np.block([[c, -s], [s, c]]))
    return np.stack(tables).astype(jnp.bfloat16)


def weighted(terms):
    total = None
    for coef, part in terms:
        if abs(coef) < 1e-12:
            continue
        value = part if coef == 1.0 else (-part if coef == -1.0 else part * coef)
        total = value if total is None else total + value
    return total


def unit(fn, b, k1, n):
    value = fn(math.pi * (b * k1 % (2 * n)) / n)
    return float(round(value)) if abs(value - round(value)) < 1e-12 else value


def front(n, rows, load, spec):
    width = spec.shape[-1] // 2
    x = [load(b) for b in range(n)]
    even, odd = range(0, n, 2), range(1, n, 2)
    for k1 in range(n // 2 + 1):
        ce = weighted([(unit(math.cos, b, k1, n), x[b]) for b in even])
        co = weighted([(unit(math.cos, b, k1, n), x[b]) for b in odd])
        se = weighted([(unit(math.sin, b, k1, n), x[b]) for b in even])
        so = weighted([(unit(math.sin, b, k1, n), x[b]) for b in odd])
        k2 = n - k1
        if k1 == k2:
            spec[k1, rows, :width] = ce.astype(bf16)
            spec[k1, rows, width:] = (-so).astype(bf16)
            continue
        spec[k1, rows, :width] = (ce + co).astype(bf16)
        spec[k2, rows, :width] = (ce - co).astype(bf16)
        if k1:
            spec[k1, rows, width:] = (-(se + so)).astype(bf16)
            spec[k2, rows, width:] = (se - so).astype(bf16)


def middle(k1, channels, real_only, spec, table, wide):
    width = table.shape[-1] // 2
    depth = width if real_only else 2 * width
    full = jnp.dot(spec[k1, : 2 * channels, :depth], table[k1, :depth, :], preferred_element_type=f32)
    ur, ui = full[:channels, :width], full[:channels, width:]
    hr, hi = full[channels:, :width], full[channels:, width:]
    prod = jnp.concatenate([ur * hr - ui * hi, ur * hi + ui * hr], axis=1).astype(bf16)
    wide[k1, :channels, :depth] = lax.dot_general(
        prod, table[k1, :depth, :], (((1,), (1,)), ((), ())), preferred_element_type=f32
    )


def back(n, rows, wide, store):
    width = wide.shape[-1] // 2
    scale = 1.0 / (2 * n * width)
    re = [wide[k, rows, :width] for k in range(n + 1)]
    im = [None if k in (0, n) else wide[k, rows, width:] for k in range(n + 1)]
    for parity in (0, 1):
        sign = 1.0 if parity == 0 else -1.0
        reals, imags = [], []
        for k in range(n // 2):
            reals.append(re[k] + re[n - k] if parity == 0 else re[k] - re[n - k])
            imags.append(None if k == 0 else (im[k] - im[n - k] if parity == 0 else im[k] + im[n - k]))
        for b in range(parity, n, 2):
            terms = []
            for k in range(n // 2):
                weight = scale if k == 0 else 2.0 * scale
                terms.append((weight * unit(math.cos, b, k, n), reals[k]))
                if k:
                    terms.append((-weight * unit(math.sin, b, k, n), imags[k]))
            if parity == 0:
                terms.append((2.0 * scale * unit(math.cos, b, n // 2, n), re[n // 2]))
            else:
                terms.append((-2.0 * scale * unit(math.sin, b, n // 2, n), im[n // 2]))
            terms = [(c if abs(c) > 1e-9 * scale else 0.0, v) for c, v in terms]
            store(b, weighted([(c / scale, v) for c, v in terms]) * scale)


ROWS = 16


def conv_kernel(n, x_ref, table, y_ref, spec, wide):
    channels = y_ref.shape[1]

    def front_step(i, _):
        rows = pl.ds(pl.multiple_of(i * ROWS, ROWS), ROWS)
        front(n, rows, lambda b: x_ref[b, rows, :].astype(f32), spec)
        return 0

    lax.fori_loop(0, 2 * channels // ROWS, front_step, 0)
    middle(0, channels, True, spec, table, wide)
    middle(n, channels, True, spec, table, wide)

    def middle_step(k1, _):
        middle(k1, channels, False, spec, table, wide)
        return 0

    lax.fori_loop(1, n, middle_step, 0)

    height = min(ROWS, channels)

    def back_step(i, _):
        rows = pl.ds(pl.multiple_of(i * height, height), height)

        def store(b, value):
            y_ref[b, rows, :] = value.astype(bf16)

        back(n, rows, wide, store)
        return 0

    lax.fori_loop(0, channels // height, back_step, 0)


def per_device_generic(signal, pre_gate, post_gate, filter_taps, skip_gain, out_weight):
    channels_here, tokens_here = signal.shape
    n = lax.axis_size("ctx")
    mine = channels_here // n
    gated_input = signal.astype(f32) * pre_gate.astype(f32)
    stacked = jnp.stack([gated_input.astype(bf16), filter_taps.astype(bf16)])
    stacked = stacked.reshape(2, n, mine, tokens_here).transpose(1, 0, 2, 3).reshape(n, 2 * mine, tokens_here)
    blocks = lax.all_to_all(stacked, "ctx", split_axis=0, concat_axis=0, tiled=True)
    table = jnp.asarray(freq_tables(n, tokens_here))
    conv = pl.pallas_call(
        functools.partial(conv_kernel, n),
        out_shape=jax.ShapeDtypeStruct((n, mine, tokens_here), bf16),
        in_specs=[pl.BlockSpec(memory_space=pltpu.VMEM)] * 2,
        out_specs=pl.BlockSpec(memory_space=pltpu.VMEM),
        scratch_shapes=[
            pltpu.VMEM((n + 1, 2 * mine, 2 * tokens_here), bf16),
            pltpu.VMEM((n + 1, mine, 2 * tokens_here), f32),
        ],
        compiler_params=pltpu.CompilerParams(vmem_limit_bytes=48 * 1024 * 1024),
    )(blocks, table)
    conv = lax.all_to_all(conv, "ctx", split_axis=0, concat_axis=0, tiled=True)
    convolved = conv.reshape(channels_here, tokens_here).astype(f32)
    mixed = (post_gate.astype(f32) * (convolved + skip_gain[:, None] * gated_input)).astype(bf16)
    return lax.psum_scatter(
        lax.dot_general(
            out_weight, mixed, (((0,), (0,)), ((), ())), preferred_element_type=f32
        ).astype(bf16),
        "tp",
        scatter_dimension=0,
        tiled=True,
    )


MESH = pl.DeviceIdType.MESH
CHUNKS = 2
SUBS = 2


def chunk_sizes(mine):
    return (mine - mine // 4, mine // 4)


def fused_kernel(
    n, sig, pre, post, taps, skip, weight_hbm, table_hbm, out,
    x_send, x_recv, spec, wide, y_send, y_recv, table, weight, mixed_t, part, a_send, a_recv, c_send, c_recv,
    load_sem, xs_sem, xr_sem, ys_sem, yr_sem, as_sem, ar_sem, cs_sem, cr_sem,
):
    me = lax.axis_index("ctx")
    tp = lax.axis_index("tp")
    row, core = tp // 2, tp % 2
    partner = row * 2 + (1 - core)
    across = (1 - row) * 2 + core
    channels, width = sig.shape
    sizes = chunk_sizes(channels // n)
    offsets = (0, sizes[0])
    feats = out.shape[0]
    far_peers = [m for m in range(1, n) if 2 * m >= n]
    near_peers = [m for m in range(1, n) if 2 * m < n]
    order = [m for i, far_peer in enumerate(far_peers) for m in [far_peer] + near_peers[i : i + 1]]
    span = width // SUBS

    def peer_of(mask):
        peer, bit = me, 1
        while bit < n:
            if mask // bit % 2:
                peer = peer + bit * (1 - 2 * ((me // bit) % 2))
            bit *= 2
        return peer


    loads = [pltpu.make_async_copy(table_hbm, table, load_sem.at[0])]
    for f in range(4):
        loads.append(
            pltpu.make_async_copy(weight_hbm.at[:, pl.ds(f * feats, feats)], weight.at[f], load_sem.at[1 + f])
        )
    barrier = pltpu.get_barrier_semaphore()
    for d in range(1, n):
        pl.semaphore_signal(barrier, inc=1, device_id={"ctx": peer_of(d)}, device_id_type=MESH)
    pl.semaphore_signal(barrier, inc=1, device_id={"tp": partner}, device_id_type=MESH)
    pl.semaphore_signal(barrier, inc=1, device_id={"tp": across}, device_id_type=MESH)

    def owned(h, peer):
        return pl.ds(pl.multiple_of(n * offsets[h] + peer * sizes[h], 16), sizes[h])

    def pair(h):
        return pl.ds(2 * offsets[h], 2 * sizes[h])

    def gated(rows):
        return sig[rows, :].astype(f32) * pre[rows, :].astype(f32)

    def fill(ref, slot, h, peer):
        rows = owned(h, peer)
        middle_row = 2 * offsets[h] + sizes[h]
        ref[slot, pl.ds(2 * offsets[h], sizes[h]), :] = gated(rows).astype(bf16)
        ref[slot, pl.ds(middle_row, sizes[h]), :] = taps[rows, :].astype(bf16)

    x_copies = {}
    for h in range(CHUNKS):
        for d in order:
            fill(x_send, d, h, peer_of(d))
        if h == 0:
            pl.semaphore_wait(barrier, n + 1)
        for d in order:
            copy = pltpu.make_async_remote_copy(
                src_ref=x_send.at[d, pair(h)],
                dst_ref=x_recv.at[me, pair(h)],
                send_sem=xs_sem.at[h, d],
                recv_sem=xr_sem.at[h, d],
                device_id={"ctx": peer_of(d)},
                device_id_type=MESH,
            )
            copy.start()
            x_copies[h, d] = copy
        for load in loads[:1] if h == 0 else loads[1:]:
            load.start()
    for h in range(CHUNKS):
        fill(x_recv, me, h, me)
    loads[0].wait()

    y_copies = {}
    skip_t = skip[...].T

    def mix(h, t):
        for d in order:
            y_copies[h, t, d].wait_recv()
        y_recv[t, owned(h, me), :] = y_send[t, me, pl.ds(offsets[h], sizes[h])]
        step = 128
        tokens = pl.ds(t * span, span)
        first = n * offsets[h] // step
        for j in range(first, first + n * sizes[h] // step):
            rows = pl.ds(j * step, step)
            gate_in = sig[rows, tokens].astype(f32) * pre[rows, tokens].astype(f32)
            conv = y_recv[t, rows, :].astype(f32)
            value = post[rows, tokens].astype(f32) * (conv + skip_t[:, j : j + 1] * gate_in)
            mixed_t[tokens, rows] = value.T.astype(bf16)

    def send_back(h, t):
        for d in order:
            peer = peer_of(d)
            copy = pltpu.make_async_remote_copy(
                src_ref=y_send.at[t, peer, pl.ds(offsets[h], sizes[h])],
                dst_ref=y_recv.at[t, owned(h, me)],
                send_sem=ys_sem.at[h, t, d],
                recv_sem=yr_sem.at[h, t, d],
                device_id={"ctx": peer},
                device_id_type=MESH,
            )
            copy.start()
            y_copies[h, t, d] = copy

    for h in range(CHUNKS):
        for d in order:
            x_copies[h, d].wait_recv()
        if h == 1:
            send_back(0, 0)
        size = sizes[h]

        def front_step(i, _):
            rows = pl.ds(pl.multiple_of(i * ROWS, ROWS), ROWS)
            source = pl.ds(pl.multiple_of(2 * offsets[h] + i * ROWS, ROWS), ROWS)
            front(n, rows, lambda b: x_recv[b, source, :].astype(f32), spec)
            return 0

        lax.fori_loop(0, 2 * size // ROWS, front_step, 0)
        middle(0, size, True, spec, table, wide)
        middle(n, size, True, spec, table, wide)

        def middle_step(k1, _):
            middle(k1, size, False, spec, table, wide)
            return 0

        lax.fori_loop(1, n, middle_step, 0, unroll=True)

        def back_step(i, _):
            rows = pl.ds(pl.multiple_of(i * ROWS, ROWS), ROWS)
            target = pl.ds(pl.multiple_of(offsets[h] + i * ROWS, ROWS), ROWS)

            def store(b, value):
                for t in range(SUBS):
                    y_send[t, b, target, :] = value[:, t * span : (t + 1) * span].astype(bf16)

            back(n, rows, wide, store)
            return 0

        lax.fori_loop(0, size // ROWS, back_step, 0)
    send_back(1, 0)
    for t in range(1, SUBS):
        send_back(0, t)
        send_back(1, t)

    for load in loads[1:]:
        load.wait()
    tile = 256
    tiles = feats // tile
    head = n * sizes[0]

    def columns(c):
        return pl.ds(pl.multiple_of(c * tile, tile), tile)

    def project(f, t, c, lo, hi):
        return jnp.dot(
            mixed_t[t * span : (t + 1) * span, lo:hi], weight[f, lo:hi, columns(c)], preferred_element_type=f32
        )

    def each_tile(body):
        def step(c, _):
            body(c)
            return 0

        lax.fori_loop(0, tiles, step, 0)

    def to_partner(slot, t):
        copy = pltpu.make_async_remote_copy(
            src_ref=a_send.at[slot, t],
            dst_ref=a_recv.at[slot, t],
            send_sem=as_sem.at[slot, t],
            recv_sem=ar_sem.at[slot, t],
            device_id={"tp": partner},
            device_id_type=MESH,
        )
        copy.start()
        return copy

    a_copies, c_copies = {}, {}
    far = (1 - row) * 2 + (1 - core)
    for t in range(SUBS):
        tokens = pl.ds(t * span, span)
        mix(0, t)

        def early(c):
            part[far, tokens, columns(c)] = project(far, t, c, 0, head)
            part[across, tokens, columns(c)] = project(across, t, c, 0, head)

        each_tile(early)
        mix(1, t)

        def far_rest(c):
            total = part[far, tokens, columns(c)] + project(far, t, c, head, channels)
            a_send[0, t, :, columns(c)] = total.astype(bf16)

        each_tile(far_rest)
        a_copies[0, t] = to_partner(0, t)

        def across_rest(c):
            part[across, tokens, columns(c)] += project(across, t, c, head, channels)

        each_tile(across_rest)
        a_copies[0, t].wait_recv()

        def across_sum(c):
            total = part[across, tokens, columns(c)] + a_recv[0, t, :, columns(c)].astype(f32)
            c_send[t, :, columns(c)] = total.astype(bf16)

        each_tile(across_sum)
        copy = pltpu.make_async_remote_copy(
            src_ref=c_send.at[t],
            dst_ref=c_recv.at[t],
            send_sem=cs_sem.at[t],
            recv_sem=cr_sem.at[t],
            device_id={"tp": across},
            device_id_type=MESH,
        )
        copy.start()
        c_copies[t] = copy

        def partner_all(c):
            a_send[1, t, :, columns(c)] = project(partner, t, c, 0, channels).astype(bf16)

        each_tile(partner_all)
        a_copies[1, t] = to_partner(1, t)

        def own_all(c):
            part[tp, tokens, columns(c)] = project(tp, t, c, 0, channels)

        each_tile(own_all)
    for t in range(SUBS):
        tokens = pl.ds(t * span, span)
        a_copies[1, t].wait_recv()
        c_copies[t].wait_recv()

        def finish(c):
            total = part[tp, tokens, columns(c)] + a_recv[1, t, :, columns(c)].astype(f32)
            total = total + c_recv[t, :, columns(c)].astype(f32)
            out[columns(c), tokens] = total.T.astype(bf16)

        each_tile(finish)
    for group in (x_copies, y_copies, a_copies, c_copies):
        for copy in group.values():
            copy.wait_send()


def per_device_fused(signal, pre_gate, post_gate, filter_taps, skip_gain, out_weight):
    channels, width = signal.shape
    n = lax.axis_size("ctx")
    feats = out_weight.shape[1] // 4
    mine = channels // n
    most = max(chunk_sizes(mine))
    span = width // SUBS
    vmem = pl.BlockSpec(memory_space=pltpu.VMEM)
    hbm = pl.BlockSpec(memory_space=pl.ANY)
    dma = pltpu.SemaphoreType.DMA
    return pl.pallas_call(
        functools.partial(fused_kernel, n),
        out_shape=jax.ShapeDtypeStruct((feats, width), bf16),
        in_specs=[vmem] * 5 + [hbm] * 2,
        out_specs=vmem,
        scratch_shapes=[
            pltpu.VMEM((n, 2 * mine, width), bf16),
            pltpu.VMEM((n, 2 * mine, width), bf16),
            pltpu.VMEM((n + 1, 2 * most, 2 * width), bf16),
            pltpu.VMEM((n + 1, most, 2 * width), f32),
            pltpu.VMEM((SUBS, n, mine, span), bf16),
            pltpu.VMEM((SUBS, channels, span), bf16),
            pltpu.VMEM((n + 1, 2 * width, 2 * width), bf16),
            pltpu.VMEM((4, channels, feats), bf16),
            pltpu.VMEM((width, channels), bf16),
            pltpu.VMEM((4, width, feats), f32),
            pltpu.VMEM((2, SUBS, span, feats), bf16),
            pltpu.VMEM((2, SUBS, span, feats), bf16),
            pltpu.VMEM((SUBS, span, feats), bf16),
            pltpu.VMEM((SUBS, span, feats), bf16),
            dma((5,)),
            dma((CHUNKS, n)),
            dma((CHUNKS, n)),
            dma((CHUNKS, SUBS, n)),
            dma((CHUNKS, SUBS, n)),
            dma((2, SUBS)),
            dma((2, SUBS)),
            dma((SUBS,)),
            dma((SUBS,)),
        ],
        compiler_params=pltpu.CompilerParams(
            collective_id=0, has_side_effects=True, vmem_limit_bytes=56 * 1024 * 1024
        ),
    )(
        signal, pre_gate, post_gate, filter_taps, skip_gain.reshape(channels // 128, 128), out_weight,
        jnp.asarray(freq_tables(n, width)),
    )


def per_device(signal, *rest):
    channels, width = signal.shape
    features = rest[-1].shape[1]
    n, tp = lax.axis_size("ctx"), lax.axis_size("tp")
    fits = n in (2, 4, 8) and tp == 4 and width % 256 == 0
    fits = fits and channels % (4 * n * 16) == 0 and channels % (4 * 128) == 0
    fits = fits and features % (4 * 256) == 0
    return (per_device_fused if fits else per_device_generic)(signal, *rest)


def solution(mesh):
    return jax.shard_map(
        per_device,
        mesh=mesh,
        in_specs=(
            P("tp", "ctx"),
            P("tp", "ctx"),
            P("tp", "ctx"),
            P("tp", "ctx"),
            P("tp"),
            P("tp", None),
        ),
        out_specs=P("tp", "ctx"),
        check_vma=False,
    )
```

```python
import functools
import math

import jax
import jax.numpy as jnp
import numpy as np
from jax import lax
from jax.experimental import pallas as pl
from jax.experimental.pallas import tpu as pltpu
from jax.sharding import PartitionSpec as P

f32 = jnp.float32
bf16 = jnp.bfloat16


def freq_tables(blocks, width):
    total = 2 * blocks * width
    place = np.arange(width, dtype=np.int64)
    tables = []
    for k1 in range(blocks + 1):
        angle = (place[:, None] * (k1 + 2 * blocks * place[None, :]) % total) * (2.0 * math.pi / total)
        c, s = np.cos(angle), np.sin(angle)
        tables.append(np.block([[c, -s], [s, c]]))
    return np.stack(tables).astype(jnp.bfloat16)


def weighted(terms):
    total = None
    for coef, part in terms:
        if abs(coef) < 1e-12:
            continue
        value = part if coef == 1.0 else (-part if coef == -1.0 else part * coef)
        total = value if total is None else total + value
    return total


def unit(fn, b, k1, n):
    value = fn(math.pi * (b * k1 % (2 * n)) / n)
    return float(round(value)) if abs(value - round(value)) < 1e-12 else value


def front(n, rows, load, spec):
    width = spec.shape[-1] // 2
    x = [load(b) for b in range(n)]
    even, odd = range(0, n, 2), range(1, n, 2)
    for k1 in range(n // 2 + 1):
        ce = weighted([(unit(math.cos, b, k1, n), x[b]) for b in even])
        co = weighted([(unit(math.cos, b, k1, n), x[b]) for b in odd])
        se = weighted([(unit(math.sin, b, k1, n), x[b]) for b in even])
        so = weighted([(unit(math.sin, b, k1, n), x[b]) for b in odd])
        k2 = n - k1
        if k1 == k2:
            spec[k1, rows, :width] = ce.astype(bf16)
            spec[k1, rows, width:] = (-so).astype(bf16)
            continue
        spec[k1, rows, :width] = (ce + co).astype(bf16)
        spec[k2, rows, :width] = (ce - co).astype(bf16)
        if k1:
            spec[k1, rows, width:] = (-(se + so)).astype(bf16)
            spec[k2, rows, width:] = (se - so).astype(bf16)


def middle(k1, channels, real_only, spec, table, wide):
    width = table.shape[-1] // 2
    depth = width if real_only else 2 * width
    full = jnp.dot(spec[k1, : 2 * channels, :depth], table[k1, :depth, :], preferred_element_type=f32)
    ur, ui = full[:channels, :width], full[:channels, width:]
    hr, hi = full[channels:, :width], full[channels:, width:]
    prod = jnp.concatenate([ur * hr - ui * hi, ur * hi + ui * hr], axis=1).astype(bf16)
    wide[k1, :channels, :depth] = lax.dot_general(
        prod, table[k1, :depth, :], (((1,), (1,)), ((), ())), preferred_element_type=f32
    )


def back(n, rows, wide, store):
    width = wide.shape[-1] // 2
    scale = 1.0 / (2 * n * width)
    re = [wide[k, rows, :width] for k in range(n + 1)]
    im = [None if k in (0, n) else wide[k, rows, width:] for k in range(n + 1)]
    for parity in (0, 1):
        sign = 1.0 if parity == 0 else -1.0
        reals, imags = [], []
        for k in range(n // 2):
            reals.append(re[k] + re[n - k] if parity == 0 else re[k] - re[n - k])
            imags.append(None if k == 0 else (im[k] - im[n - k] if parity == 0 else im[k] + im[n - k]))
        for b in range(parity, n, 2):
            terms = []
            for k in range(n // 2):
                weight = scale if k == 0 else 2.0 * scale
                terms.append((weight * unit(math.cos, b, k, n), reals[k]))
                if k:
                    terms.append((-weight * unit(math.sin, b, k, n), imags[k]))
            if parity == 0:
                terms.append((2.0 * scale * unit(math.cos, b, n // 2, n), re[n // 2]))
            else:
                terms.append((-2.0 * scale * unit(math.sin, b, n // 2, n), im[n // 2]))
            terms = [(c if abs(c) > 1e-9 * scale else 0.0, v) for c, v in terms]
            store(b, weighted([(c / scale, v) for c, v in terms]) * scale)


ROWS = 16


def conv_kernel(n, x_ref, table, y_ref, spec, wide):
    channels = y_ref.shape[1]

    def front_step(i, _):
        rows = pl.ds(pl.multiple_of(i * ROWS, ROWS), ROWS)
        front(n, rows, lambda b: x_ref[b, rows, :].astype(f32), spec)
        return 0

    lax.fori_loop(0, 2 * channels // ROWS, front_step, 0)
    middle(0, channels, True, spec, table, wide)
    middle(n, channels, True, spec, table, wide)

    def middle_step(k1, _):
        middle(k1, channels, False, spec, table, wide)
        return 0

    lax.fori_loop(1, n, middle_step, 0)

    height = min(ROWS, channels)

    def back_step(i, _):
        rows = pl.ds(pl.multiple_of(i * height, height), height)

        def store(b, value):
            y_ref[b, rows, :] = value.astype(bf16)

        back(n, rows, wide, store)
        return 0

    lax.fori_loop(0, channels // height, back_step, 0)


def per_device_generic(signal, pre_gate, post_gate, filter_taps, skip_gain, out_weight):
    channels_here, tokens_here = signal.shape
    n = lax.axis_size("ctx")
    mine = channels_here // n
    gated_input = signal.astype(f32) * pre_gate.astype(f32)
    stacked = jnp.stack([gated_input.astype(bf16), filter_taps.astype(bf16)])
    stacked = stacked.reshape(2, n, mine, tokens_here).transpose(1, 0, 2, 3).reshape(n, 2 * mine, tokens_here)
    blocks = lax.all_to_all(stacked, "ctx", split_axis=0, concat_axis=0, tiled=True)
    table = jnp.asarray(freq_tables(n, tokens_here))
    conv = pl.pallas_call(
        functools.partial(conv_kernel, n),
        out_shape=jax.ShapeDtypeStruct((n, mine, tokens_here), bf16),
        in_specs=[pl.BlockSpec(memory_space=pltpu.VMEM)] * 2,
        out_specs=pl.BlockSpec(memory_space=pltpu.VMEM),
        scratch_shapes=[
            pltpu.VMEM((n + 1, 2 * mine, 2 * tokens_here), bf16),
            pltpu.VMEM((n + 1, mine, 2 * tokens_here), f32),
        ],
        compiler_params=pltpu.CompilerParams(vmem_limit_bytes=48 * 1024 * 1024),
    )(blocks, table)
    conv = lax.all_to_all(conv, "ctx", split_axis=0, concat_axis=0, tiled=True)
    convolved = conv.reshape(channels_here, tokens_here).astype(f32)
    mixed = (post_gate.astype(f32) * (convolved + skip_gain[:, None] * gated_input)).astype(bf16)
    return lax.psum_scatter(
        lax.dot_general(
            out_weight, mixed, (((0,), (0,)), ((), ())), preferred_element_type=f32
        ).astype(bf16),
        "tp",
        scatter_dimension=0,
        tiled=True,
    )


MESH = pl.DeviceIdType.MESH
CHUNKS = 2
SUBS = 2
PIECES = 2


def chunk_sizes(mine):
    return (mine - mine // 4, mine // 4)


def fused_kernel(
    n, sig_hbm, pre_hbm, post_hbm, taps_hbm, skip, weight_hbm, table_hbm, out,
    sig, pre, post, taps, x_send, x_recv, spec, wide, y_send, y_recv, table, weight, mixed_t, part, a_send, a_recv, c_send, c_recv,
    in_sem, load_sem, xs_sem, xr_sem, ys_sem, yr_sem, as_sem, ar_sem, cs_sem, cr_sem,
):
    me = lax.axis_index("ctx")
    tp = lax.axis_index("tp")
    row, core = tp // 2, tp % 2
    partner = row * 2 + (1 - core)
    across = (1 - row) * 2 + core
    channels, width = sig.shape
    sizes = chunk_sizes(channels // n)
    offsets = (0, sizes[0])
    feats = out.shape[0]
    far_peers = [m for m in range(1, n) if 2 * m >= n]
    near_peers = [m for m in range(1, n) if 2 * m < n]
    order = [m for i, far_peer in enumerate(far_peers) for m in [far_peer] + near_peers[i : i + 1]]
    span = width // SUBS

    def peer_of(mask):
        peer, bit = me, 1
        while bit < n:
            if mask // bit % 2:
                peer = peer + bit * (1 - 2 * ((me // bit) % 2))
            bit *= 2
        return peer


    in_loads = []
    for h in range(CHUNKS):
        rows = pl.ds(n * offsets[h], n * sizes[h])
        pairs = ((sig_hbm, sig), (pre_hbm, pre), (taps_hbm, taps), (post_hbm, post))
        in_loads.append(
            [
                pltpu.make_async_copy(source.at[rows], target.at[rows], in_sem.at[h, i])
                for i, (source, target) in enumerate(pairs)
            ]
        )
        for load in in_loads[h][:3]:
            load.start()
    loads = [pltpu.make_async_copy(table_hbm, table, load_sem.at[0])]
    for f in range(4):
        loads.append(
            pltpu.make_async_copy(weight_hbm.at[:, pl.ds(f * feats, feats)], weight.at[f], load_sem.at[1 + f])
        )
    barrier = pltpu.get_barrier_semaphore()
    for d in range(1, n):
        pl.semaphore_signal(barrier, inc=1, device_id={"ctx": peer_of(d)}, device_id_type=MESH)
    pl.semaphore_signal(barrier, inc=1, device_id={"tp": partner}, device_id_type=MESH)
    pl.semaphore_signal(barrier, inc=1, device_id={"tp": across}, device_id_type=MESH)

    def owned(h, peer):
        return pl.ds(pl.multiple_of(n * offsets[h] + peer * sizes[h], 16), sizes[h])

    def pair(h):
        return pl.ds(2 * offsets[h], 2 * sizes[h])

    def gated(rows):
        return sig[rows, :].astype(f32) * pre[rows, :].astype(f32)

    def fill(ref, slot, h, peer):
        rows = owned(h, peer)
        middle_row = 2 * offsets[h] + sizes[h]
        ref[slot, pl.ds(2 * offsets[h], sizes[h]), :] = gated(rows).astype(bf16)
        ref[slot, pl.ds(middle_row, sizes[h]), :] = taps[rows, :].astype(bf16)

    x_copies = {}
    for h in range(CHUNKS):
        for load in in_loads[h][:3]:
            load.wait()
        for d in order:
            fill(x_send, d, h, peer_of(d))
        if h == 0:
            pl.semaphore_wait(barrier, n + 1)
        for d in order:
            copy = pltpu.make_async_remote_copy(
                src_ref=x_send.at[d, pair(h)],
                dst_ref=x_recv.at[me, pair(h)],
                send_sem=xs_sem.at[h, d],
                recv_sem=xr_sem.at[h, d],
                device_id={"ctx": peer_of(d)},
                device_id_type=MESH,
            )
            copy.start()
            x_copies[h, d] = copy
        for load in loads[:1] if h == 0 else loads[1:]:
            load.start()
        in_loads[h][3].start()
    for h in range(CHUNKS):
        fill(x_recv, me, h, me)
    loads[0].wait()

    y_copies = {}
    skip_t = skip[...].T

    def mix(h, t):
        for d in order:
            y_copies[h, t, d].wait_recv()
        y_recv[t, owned(h, me), :] = y_send[t, me, pl.ds(offsets[h], sizes[h])]
        step = 128
        tokens = pl.ds(t * span, span)
        first = n * offsets[h] // step
        for j in range(first, first + n * sizes[h] // step):
            rows = pl.ds(j * step, step)
            gate_in = sig[rows, tokens].astype(f32) * pre[rows, tokens].astype(f32)
            conv = y_recv[t, rows, :].astype(f32)
            value = post[rows, tokens].astype(f32) * (conv + skip_t[:, j : j + 1] * gate_in)
            mixed_t[tokens, rows] = value.T.astype(bf16)

    def send_back(h, t):
        for d in order:
            peer = peer_of(d)
            copy = pltpu.make_async_remote_copy(
                src_ref=y_send.at[t, peer, pl.ds(offsets[h], sizes[h])],
                dst_ref=y_recv.at[t, owned(h, me)],
                send_sem=ys_sem.at[h, t, d],
                recv_sem=yr_sem.at[h, t, d],
                device_id={"ctx": peer},
                device_id_type=MESH,
            )
            copy.start()
            y_copies[h, t, d] = copy

    for h in range(CHUNKS):
        for d in order:
            x_copies[h, d].wait_recv()
        if h == 1:
            send_back(0, 0)
        size = sizes[h]

        def front_step(i, _):
            rows = pl.ds(pl.multiple_of(i * ROWS, ROWS), ROWS)
            source = pl.ds(pl.multiple_of(2 * offsets[h] + i * ROWS, ROWS), ROWS)
            front(n, rows, lambda b: x_recv[b, source, :].astype(f32), spec)
            return 0

        lax.fori_loop(0, 2 * size // ROWS, front_step, 0)
        middle(0, size, True, spec, table, wide)
        middle(n, size, True, spec, table, wide)

        def middle_step(k1, _):
            middle(k1, size, False, spec, table, wide)
            return 0

        lax.fori_loop(1, n, middle_step, 0, unroll=True)

        def back_step(i, _):
            rows = pl.ds(pl.multiple_of(i * ROWS, ROWS), ROWS)
            target = pl.ds(pl.multiple_of(offsets[h] + i * ROWS, ROWS), ROWS)

            def store(b, value):
                for t in range(SUBS):
                    y_send[t, b, target, :] = value[:, t * span : (t + 1) * span].astype(bf16)

            back(n, rows, wide, store)
            return 0

        lax.fori_loop(0, size // ROWS, back_step, 0)
    send_back(1, 0)
    for t in range(1, SUBS):
        send_back(0, t)
        send_back(1, t)

    for load in loads[1:] + [in_loads[h][3] for h in range(CHUNKS)]:
        load.wait()
    tile = 256
    tiles = feats // tile
    head = n * sizes[0]

    def columns(c):
        return pl.ds(pl.multiple_of(c * tile, tile), tile)

    def project(f, tokens, c, lo, hi):
        return jnp.dot(mixed_t[tokens, lo:hi], weight[f, lo:hi, columns(c)], preferred_element_type=f32)

    def each_tile(body, piece=None):
        def step(c, _):
            body(c)
            return 0

        lo, hi = (0, tiles) if piece is None else (piece * tiles // PIECES, (piece + 1) * tiles // PIECES)
        lax.fori_loop(lo, hi, step, 0)

    def reduce_copy(send, recv, send_sems, recv_sems, at, piece, target):
        cut = pl.ds(piece * (feats // PIECES), feats // PIECES)
        copy = pltpu.make_async_remote_copy(
            src_ref=send.at[(*at, slice(None), cut)],
            dst_ref=recv.at[(*at, slice(None), cut)],
            send_sem=send_sems.at[(*at, piece)],
            recv_sem=recv_sems.at[(*at, piece)],
            device_id={"tp": target},
            device_id_type=MESH,
        )
        copy.start()
        return copy

    a_copies, c_copies = {}, {}
    far = (1 - row) * 2 + (1 - core)
    for t in range(SUBS):
        tokens = pl.ds(t * span, span)
        mix(0, t)

        def early(c):
            part[far, tokens, columns(c)] = project(far, tokens, c, 0, head)
            part[across, tokens, columns(c)] = project(across, tokens, c, 0, head)

        each_tile(early)
        mix(1, t)

        def far_rest(c):
            total = part[far, tokens, columns(c)] + project(far, tokens, c, head, channels)
            a_send[0, t, :, columns(c)] = total.astype(bf16)

        for piece in range(PIECES):
            each_tile(far_rest, piece)
            a_copies[0, t, piece] = reduce_copy(a_send, a_recv, as_sem, ar_sem, (0, t), piece, partner)

        def across_rest(c):
            part[across, tokens, columns(c)] += project(across, tokens, c, head, channels)

        each_tile(across_rest)

        def across_sum(c):
            total = part[across, tokens, columns(c)] + a_recv[0, t, :, columns(c)].astype(f32)
            c_send[t, :, columns(c)] = total.astype(bf16)

        for piece in range(PIECES):
            a_copies[0, t, piece].wait_recv()
            each_tile(across_sum, piece)
            c_copies[t, piece] = reduce_copy(c_send, c_recv, cs_sem, cr_sem, (t,), piece, across)

    def partner_all(c):
        total = project(partner, pl.ds(0, width), c, 0, channels).astype(bf16)
        for t in range(SUBS):
            a_send[1, t, :, columns(c)] = total[t * span : (t + 1) * span]

    for piece in range(PIECES):
        each_tile(partner_all, piece)
        for t in range(SUBS):
            a_copies[1, t, piece] = reduce_copy(a_send, a_recv, as_sem, ar_sem, (1, t), piece, partner)

    def own_all(c):
        part[tp, :, columns(c)] = project(tp, pl.ds(0, width), c, 0, channels)

    each_tile(own_all)
    for t in range(SUBS):
        for piece in range(PIECES):
            a_copies[1, t, piece].wait_recv()
        tokens = pl.ds(t * span, span)

        def own_sum(c):
            part[tp, tokens, columns(c)] += a_recv[1, t, :, columns(c)].astype(f32)

        each_tile(own_sum)
    for t in range(SUBS):
        tokens = pl.ds(t * span, span)

        def finish(c):
            total = part[tp, tokens, columns(c)] + c_recv[t, :, columns(c)].astype(f32)
            out[columns(c), tokens] = total.T.astype(bf16)

        for piece in range(PIECES):
            c_copies[t, piece].wait_recv()
            each_tile(finish, piece)
    for group in (x_copies, y_copies, a_copies, c_copies):
        for copy in group.values():
            copy.wait_send()


def per_device_fused(signal, pre_gate, post_gate, filter_taps, skip_gain, out_weight):
    channels, width = signal.shape
    n = lax.axis_size("ctx")
    feats = out_weight.shape[1] // 4
    mine = channels // n
    most = max(chunk_sizes(mine))
    span = width // SUBS
    vmem = pl.BlockSpec(memory_space=pltpu.VMEM)
    hbm = pl.BlockSpec(memory_space=pl.ANY)
    dma = pltpu.SemaphoreType.DMA
    return pl.pallas_call(
        functools.partial(fused_kernel, n),
        out_shape=jax.ShapeDtypeStruct((feats, width), bf16),
        in_specs=[hbm] * 4 + [vmem] + [hbm] * 2,
        out_specs=vmem,
        scratch_shapes=[
            pltpu.VMEM((channels, width), bf16),
            pltpu.VMEM((channels, width), bf16),
            pltpu.VMEM((channels, width), bf16),
            pltpu.VMEM((channels, width), f32),
            pltpu.VMEM((n, 2 * mine, width), bf16),
            pltpu.VMEM((n, 2 * mine, width), bf16),
            pltpu.VMEM((n + 1, 2 * most, 2 * width), bf16),
            pltpu.VMEM((n + 1, most, 2 * width), f32),
            pltpu.VMEM((SUBS, n, mine, span), bf16),
            pltpu.VMEM((SUBS, channels, span), bf16),
            pltpu.VMEM((n + 1, 2 * width, 2 * width), bf16),
            pltpu.VMEM((4, channels, feats), bf16),
            pltpu.VMEM((width, channels), bf16),
            pltpu.VMEM((4, width, feats), f32),
            pltpu.VMEM((2, SUBS, span, feats), bf16),
            pltpu.VMEM((2, SUBS, span, feats), bf16),
            pltpu.VMEM((SUBS, span, feats), bf16),
            pltpu.VMEM((SUBS, span, feats), bf16),
            dma((CHUNKS, 4)),
            dma((5,)),
            dma((CHUNKS, n)),
            dma((CHUNKS, n)),
            dma((CHUNKS, SUBS, n)),
            dma((CHUNKS, SUBS, n)),
            dma((2, SUBS, PIECES)),
            dma((2, SUBS, PIECES)),
            dma((SUBS, PIECES)),
            dma((SUBS, PIECES)),
        ],
        compiler_params=pltpu.CompilerParams(
            collective_id=0, has_side_effects=True, vmem_limit_bytes=56 * 1024 * 1024
        ),
    )(
        signal, pre_gate, post_gate, filter_taps, skip_gain.reshape(channels // 128, 128), out_weight,
        jnp.asarray(freq_tables(n, width)),
    )


def per_device(signal, *rest):
    channels, width = signal.shape
    features = rest[-1].shape[1]
    n, tp = lax.axis_size("ctx"), lax.axis_size("tp")
    fits = n in (2, 4, 8) and tp == 4 and width % 256 == 0
    fits = fits and channels % (4 * n * 16) == 0 and channels % (4 * 128) == 0
    fits = fits and features % (4 * PIECES * 256) == 0
    return (per_device_fused if fits else per_device_generic)(signal, *rest)


def solution(mesh):
    return jax.shard_map(
        per_device,
        mesh=mesh,
        in_specs=(
            P("tp", "ctx"),
            P("tp", "ctx"),
            P("tp", "ctx"),
            P("tp", "ctx"),
            P("tp"),
            P("tp", None),
        ),
        out_specs=P("tp", "ctx"),
        check_vma=False,
    )
```

```python
import functools
import math

import jax
import jax.numpy as jnp
import numpy as np
from jax import lax
from jax.experimental import pallas as pl
from jax.experimental.pallas import tpu as pltpu
from jax.sharding import PartitionSpec as P

f32 = jnp.float32
bf16 = jnp.bfloat16


def freq_tables(blocks, width):
    total = 2 * blocks * width
    place = np.arange(width, dtype=np.int64)
    tables = []
    for k1 in range(blocks + 1):
        angle = (place[:, None] * (k1 + 2 * blocks * place[None, :]) % total) * (2.0 * math.pi / total)
        c, s = np.cos(angle), np.sin(angle)
        tables.append(np.block([[c, -s], [s, c]]))
    return np.stack(tables).astype(jnp.bfloat16)


def weighted(terms):
    total = None
    for coef, part in terms:
        if abs(coef) < 1e-12:
            continue
        value = part if coef == 1.0 else (-part if coef == -1.0 else part * coef)
        total = value if total is None else total + value
    return total


def unit(fn, b, k1, n):
    value = fn(math.pi * (b * k1 % (2 * n)) / n)
    return float(round(value)) if abs(value - round(value)) < 1e-12 else value


def front(n, rows, load, spec):
    width = spec.shape[-1] // 2
    x = [load(b) for b in range(n)]
    even, odd = range(0, n, 2), range(1, n, 2)
    for k1 in range(n // 2 + 1):
        ce = weighted([(unit(math.cos, b, k1, n), x[b]) for b in even])
        co = weighted([(unit(math.cos, b, k1, n), x[b]) for b in odd])
        se = weighted([(unit(math.sin, b, k1, n), x[b]) for b in even])
        so = weighted([(unit(math.sin, b, k1, n), x[b]) for b in odd])
        k2 = n - k1
        if k1 == k2:
            spec[k1, rows, :width] = ce.astype(bf16)
            spec[k1, rows, width:] = (-so).astype(bf16)
            continue
        spec[k1, rows, :width] = (ce + co).astype(bf16)
        spec[k2, rows, :width] = (ce - co).astype(bf16)
        if k1:
            spec[k1, rows, width:] = (-(se + so)).astype(bf16)
            spec[k2, rows, width:] = (se - so).astype(bf16)


def middle(k1, channels, real_only, spec, table, wide):
    width = table.shape[-1] // 2
    depth = width if real_only else 2 * width
    full = jnp.dot(spec[k1, : 2 * channels, :depth], table[k1, :depth, :], preferred_element_type=f32)
    ur, ui = full[:channels, :width], full[:channels, width:]
    hr, hi = full[channels:, :width], full[channels:, width:]
    prod = jnp.concatenate([ur * hr - ui * hi, ur * hi + ui * hr], axis=1).astype(bf16)
    wide[k1, :channels, :depth] = lax.dot_general(
        prod, table[k1, :depth, :], (((1,), (1,)), ((), ())), preferred_element_type=f32
    )


def back(n, rows, wide, store):
    width = wide.shape[-1] // 2
    scale = 1.0 / (2 * n * width)
    re = [wide[k, rows, :width] for k in range(n + 1)]
    im = [None if k in (0, n) else wide[k, rows, width:] for k in range(n + 1)]
    for parity in (0, 1):
        sign = 1.0 if parity == 0 else -1.0
        reals, imags = [], []
        for k in range(n // 2):
            reals.append(re[k] + re[n - k] if parity == 0 else re[k] - re[n - k])
            imags.append(None if k == 0 else (im[k] - im[n - k] if parity == 0 else im[k] + im[n - k]))
        for b in range(parity, n, 2):
            terms = []
            for k in range(n // 2):
                weight = scale if k == 0 else 2.0 * scale
                terms.append((weight * unit(math.cos, b, k, n), reals[k]))
                if k:
                    terms.append((-weight * unit(math.sin, b, k, n), imags[k]))
            if parity == 0:
                terms.append((2.0 * scale * unit(math.cos, b, n // 2, n), re[n // 2]))
            else:
                terms.append((-2.0 * scale * unit(math.sin, b, n // 2, n), im[n // 2]))
            terms = [(c if abs(c) > 1e-9 * scale else 0.0, v) for c, v in terms]
            store(b, weighted([(c / scale, v) for c, v in terms]) * scale)


ROWS = 16


def conv_kernel(n, x_ref, table, y_ref, spec, wide):
    channels = y_ref.shape[1]

    def front_step(i, _):
        rows = pl.ds(pl.multiple_of(i * ROWS, ROWS), ROWS)
        front(n, rows, lambda b: x_ref[b, rows, :].astype(f32), spec)
        return 0

    lax.fori_loop(0, 2 * channels // ROWS, front_step, 0)
    middle(0, channels, True, spec, table, wide)
    middle(n, channels, True, spec, table, wide)

    def middle_step(k1, _):
        middle(k1, channels, False, spec, table, wide)
        return 0

    lax.fori_loop(1, n, middle_step, 0)

    height = min(ROWS, channels)

    def back_step(i, _):
        rows = pl.ds(pl.multiple_of(i * height, height), height)

        def store(b, value):
            y_ref[b, rows, :] = value.astype(bf16)

        back(n, rows, wide, store)
        return 0

    lax.fori_loop(0, channels // height, back_step, 0)


def per_device_generic(signal, pre_gate, post_gate, filter_taps, skip_gain, out_weight):
    channels_here, tokens_here = signal.shape
    n = lax.axis_size("ctx")
    mine = channels_here // n
    gated_input = signal.astype(f32) * pre_gate.astype(f32)
    stacked = jnp.stack([gated_input.astype(bf16), filter_taps.astype(bf16)])
    stacked = stacked.reshape(2, n, mine, tokens_here).transpose(1, 0, 2, 3).reshape(n, 2 * mine, tokens_here)
    blocks = lax.all_to_all(stacked, "ctx", split_axis=0, concat_axis=0, tiled=True)
    table = jnp.asarray(freq_tables(n, tokens_here))
    conv = pl.pallas_call(
        functools.partial(conv_kernel, n),
        out_shape=jax.ShapeDtypeStruct((n, mine, tokens_here), bf16),
        in_specs=[pl.BlockSpec(memory_space=pltpu.VMEM)] * 2,
        out_specs=pl.BlockSpec(memory_space=pltpu.VMEM),
        scratch_shapes=[
            pltpu.VMEM((n + 1, 2 * mine, 2 * tokens_here), bf16),
            pltpu.VMEM((n + 1, mine, 2 * tokens_here), f32),
        ],
        compiler_params=pltpu.CompilerParams(vmem_limit_bytes=48 * 1024 * 1024),
    )(blocks, table)
    conv = lax.all_to_all(conv, "ctx", split_axis=0, concat_axis=0, tiled=True)
    convolved = conv.reshape(channels_here, tokens_here).astype(f32)
    mixed = (post_gate.astype(f32) * (convolved + skip_gain[:, None] * gated_input)).astype(bf16)
    return lax.psum_scatter(
        lax.dot_general(
            out_weight, mixed, (((0,), (0,)), ((), ())), preferred_element_type=f32
        ).astype(bf16),
        "tp",
        scatter_dimension=0,
        tiled=True,
    )


MESH = pl.DeviceIdType.MESH
CHUNKS = 2
SUBS = 2
PIECES = 2


def chunk_sizes(mine):
    return (mine - mine // 4, mine // 4)


def fused_kernel(
    n, sig_hbm, pre_hbm, post_hbm, taps_hbm, skip, weight_hbm, table_hbm, out_any,
    out, sig, pre, post, taps, x_send, x_recv, spec, wide, y_send, y_recv, table, weight, mixed_t, part, a_send, a_recv, c_send, c_recv,
    out_sem, in_sem, load_sem, xs_sem, xr_sem, ys_sem, yr_sem, as_sem, ar_sem, cs_sem, cr_sem,
):
    me = lax.axis_index("ctx")
    tp = lax.axis_index("tp")
    row, core = tp // 2, tp % 2
    partner = row * 2 + (1 - core)
    across = (1 - row) * 2 + core
    channels, width = sig.shape
    sizes = chunk_sizes(channels // n)
    offsets = (0, sizes[0])
    feats = out.shape[0]
    far_peers = [m for m in range(1, n) if 2 * m >= n]
    near_peers = [m for m in range(1, n) if 2 * m < n]
    order = [m for i, far_peer in enumerate(far_peers) for m in [far_peer] + near_peers[i : i + 1]]
    span = width // SUBS

    def peer_of(mask):
        peer, bit = me, 1
        while bit < n:
            if mask // bit % 2:
                peer = peer + bit * (1 - 2 * ((me // bit) % 2))
            bit *= 2
        return peer


    in_loads = []
    for h in range(CHUNKS):
        rows = pl.ds(n * offsets[h], n * sizes[h])
        pairs = ((sig_hbm, sig), (pre_hbm, pre), (taps_hbm, taps), (post_hbm, post))
        in_loads.append(
            [
                pltpu.make_async_copy(source.at[rows], target.at[rows], in_sem.at[h, i])
                for i, (source, target) in enumerate(pairs)
            ]
        )
        for load in in_loads[h][:3]:
            load.start()
    loads = [pltpu.make_async_copy(table_hbm, table, load_sem.at[0])]
    for f in range(4):
        loads.append(
            pltpu.make_async_copy(weight_hbm.at[:, pl.ds(f * feats, feats)], weight.at[f], load_sem.at[1 + f])
        )
    barrier = pltpu.get_barrier_semaphore()
    for d in range(1, n):
        pl.semaphore_signal(barrier, inc=1, device_id={"ctx": peer_of(d)}, device_id_type=MESH)
    pl.semaphore_signal(barrier, inc=1, device_id={"tp": partner}, device_id_type=MESH)
    pl.semaphore_signal(barrier, inc=1, device_id={"tp": across}, device_id_type=MESH)

    def owned(h, peer):
        return pl.ds(pl.multiple_of(n * offsets[h] + peer * sizes[h], 16), sizes[h])

    def pair(h):
        return pl.ds(2 * offsets[h], 2 * sizes[h])

    def gated(rows):
        return sig[rows, :].astype(f32) * pre[rows, :].astype(f32)

    def fill(ref, slot, h, peer):
        rows = owned(h, peer)
        middle_row = 2 * offsets[h] + sizes[h]
        ref[slot, pl.ds(2 * offsets[h], sizes[h]), :] = gated(rows).astype(bf16)
        ref[slot, pl.ds(middle_row, sizes[h]), :] = taps[rows, :].astype(bf16)

    x_copies = {}
    for h in range(CHUNKS):
        for load in in_loads[h][:3]:
            load.wait()
        for d in order:
            fill(x_send, d, h, peer_of(d))
        if h == 0:
            pl.semaphore_wait(barrier, n + 1)
        for d in order:
            copy = pltpu.make_async_remote_copy(
                src_ref=x_send.at[d, pair(h)],
                dst_ref=x_recv.at[me, pair(h)],
                send_sem=xs_sem.at[h, d],
                recv_sem=xr_sem.at[h, d],
                device_id={"ctx": peer_of(d)},
                device_id_type=MESH,
            )
            copy.start()
            x_copies[h, d] = copy
        for load in loads[:1] if h == 0 else loads[1:]:
            load.start()
        in_loads[h][3].start()
    for h in range(CHUNKS):
        fill(x_recv, me, h, me)
    loads[0].wait()

    y_copies = {}
    skip_t = skip[...].T

    def mix(h, t):
        for d in order:
            y_copies[h, t, d].wait_recv()
        y_recv[t, owned(h, me), :] = y_send[t, me, pl.ds(offsets[h], sizes[h])]
        step = 128
        tokens = pl.ds(t * span, span)
        first = n * offsets[h] // step
        for j in range(first, first + n * sizes[h] // step):
            rows = pl.ds(j * step, step)
            gate_in = sig[rows, tokens].astype(f32) * pre[rows, tokens].astype(f32)
            conv = y_recv[t, rows, :].astype(f32)
            value = post[rows, tokens].astype(f32) * (conv + skip_t[:, j : j + 1] * gate_in)
            mixed_t[tokens, rows] = value.T.astype(bf16)

    def send_back(h, t):
        for d in order:
            peer = peer_of(d)
            copy = pltpu.make_async_remote_copy(
                src_ref=y_send.at[t, peer, pl.ds(offsets[h], sizes[h])],
                dst_ref=y_recv.at[t, owned(h, me)],
                send_sem=ys_sem.at[h, t, d],
                recv_sem=yr_sem.at[h, t, d],
                device_id={"ctx": peer},
                device_id_type=MESH,
            )
            copy.start()
            y_copies[h, t, d] = copy

    for h in range(CHUNKS):
        for d in order:
            x_copies[h, d].wait_recv()
        if h == 1:
            send_back(0, 0)
        size = sizes[h]

        def front_step(i, _):
            rows = pl.ds(pl.multiple_of(i * ROWS, ROWS), ROWS)
            source = pl.ds(pl.multiple_of(2 * offsets[h] + i * ROWS, ROWS), ROWS)
            front(n, rows, lambda b: x_recv[b, source, :].astype(f32), spec)
            return 0

        lax.fori_loop(0, 2 * size // ROWS, front_step, 0)
        middle(0, size, True, spec, table, wide)
        middle(n, size, True, spec, table, wide)

        def middle_step(k1, _):
            middle(k1, size, False, spec, table, wide)
            return 0

        lax.fori_loop(1, n, middle_step, 0, unroll=True)

        def back_step(i, _):
            rows = pl.ds(pl.multiple_of(i * ROWS, ROWS), ROWS)
            target = pl.ds(pl.multiple_of(offsets[h] + i * ROWS, ROWS), ROWS)

            def store(b, value):
                for t in range(SUBS):
                    y_send[t, b, target, :] = value[:, t * span : (t + 1) * span].astype(bf16)

            back(n, rows, wide, store)
            return 0

        lax.fori_loop(0, size // ROWS, back_step, 0)
    send_back(1, 0)
    for t in range(1, SUBS):
        send_back(0, t)
        send_back(1, t)

    for load in loads[1:] + [in_loads[h][3] for h in range(CHUNKS)]:
        load.wait()
    tile = 256
    tiles = feats // tile
    head = n * sizes[0]

    def columns(c):
        return pl.ds(pl.multiple_of(c * tile, tile), tile)

    def project(f, tokens, c, lo, hi):
        return jnp.dot(mixed_t[tokens, lo:hi], weight[f, lo:hi, columns(c)], preferred_element_type=f32)

    def each_tile(body, piece=None):
        def step(c, _):
            body(c)
            return 0

        lo, hi = (0, tiles) if piece is None else (piece * tiles // PIECES, (piece + 1) * tiles // PIECES)
        lax.fori_loop(lo, hi, step, 0)

    def reduce_copy(send, recv, send_sems, recv_sems, at, piece, target):
        cut = pl.ds(piece * (feats // PIECES), feats // PIECES)
        copy = pltpu.make_async_remote_copy(
            src_ref=send.at[(*at, slice(None), cut)],
            dst_ref=recv.at[(*at, slice(None), cut)],
            send_sem=send_sems.at[(*at, piece)],
            recv_sem=recv_sems.at[(*at, piece)],
            device_id={"tp": target},
            device_id_type=MESH,
        )
        copy.start()
        return copy

    a_copies, c_copies, out_copies = {}, {}, []
    far = (1 - row) * 2 + (1 - core)
    for t in range(SUBS):
        tokens = pl.ds(t * span, span)
        mix(0, t)

        def early(c):
            part[far, tokens, columns(c)] = project(far, tokens, c, 0, head)
            part[across, tokens, columns(c)] = project(across, tokens, c, 0, head)

        each_tile(early)
        mix(1, t)

        def far_rest(c):
            total = part[far, tokens, columns(c)] + project(far, tokens, c, head, channels)
            a_send[0, t, :, columns(c)] = total.astype(bf16)

        for piece in range(PIECES):
            each_tile(far_rest, piece)
            a_copies[0, t, piece] = reduce_copy(a_send, a_recv, as_sem, ar_sem, (0, t), piece, partner)

        def across_rest(c):
            part[across, tokens, columns(c)] += project(across, tokens, c, head, channels)

        each_tile(across_rest)

        def across_sum(c):
            total = part[across, tokens, columns(c)] + a_recv[0, t, :, columns(c)].astype(f32)
            c_send[t, :, columns(c)] = total.astype(bf16)

        for piece in range(PIECES):
            a_copies[0, t, piece].wait_recv()
            each_tile(across_sum, piece)
            c_copies[t, piece] = reduce_copy(c_send, c_recv, cs_sem, cr_sem, (t,), piece, across)

    def partner_all(c):
        total = project(partner, pl.ds(0, width), c, 0, channels).astype(bf16)
        for t in range(SUBS):
            a_send[1, t, :, columns(c)] = total[t * span : (t + 1) * span]

    for piece in range(PIECES):
        each_tile(partner_all, piece)
        for t in range(SUBS):
            a_copies[1, t, piece] = reduce_copy(a_send, a_recv, as_sem, ar_sem, (1, t), piece, partner)

    def own_all(c):
        part[tp, :, columns(c)] = project(tp, pl.ds(0, width), c, 0, channels)

    each_tile(own_all)
    for t in range(SUBS):
        for piece in range(PIECES):
            a_copies[1, t, piece].wait_recv()
        tokens = pl.ds(t * span, span)

        def own_sum(c):
            part[tp, tokens, columns(c)] += a_recv[1, t, :, columns(c)].astype(f32)

        each_tile(own_sum)
    for t in range(SUBS):
        tokens = pl.ds(t * span, span)

        def finish(c):
            total = part[tp, tokens, columns(c)] + c_recv[t, :, columns(c)].astype(f32)
            out[columns(c), tokens] = total.T.astype(bf16)

        for piece in range(PIECES):
            c_copies[t, piece].wait_recv()
            each_tile(finish, piece)
            rows = pl.ds(piece * (feats // PIECES), feats // PIECES)
            copy = pltpu.make_async_copy(out.at[rows, tokens], out_any.at[rows, tokens], out_sem.at[t, piece])
            copy.start()
            out_copies.append(copy)
    for copy in out_copies:
        copy.wait()
    for group in (x_copies, y_copies, a_copies, c_copies):
        for copy in group.values():
            copy.wait_send()


def per_device_fused(signal, pre_gate, post_gate, filter_taps, skip_gain, out_weight):
    channels, width = signal.shape
    n = lax.axis_size("ctx")
    feats = out_weight.shape[1] // 4
    mine = channels // n
    most = max(chunk_sizes(mine))
    span = width // SUBS
    vmem = pl.BlockSpec(memory_space=pltpu.VMEM)
    hbm = pl.BlockSpec(memory_space=pltpu.HBM)
    dma = pltpu.SemaphoreType.DMA
    return pl.pallas_call(
        functools.partial(fused_kernel, n),
        out_shape=jax.ShapeDtypeStruct((feats, width), bf16),
        in_specs=[hbm] * 4 + [vmem] + [hbm] * 2,
        out_specs=pl.BlockSpec(memory_space=pl.ANY),
        scratch_shapes=[
            pltpu.VMEM((feats, width), bf16),
            pltpu.VMEM((channels, width), bf16),
            pltpu.VMEM((channels, width), bf16),
            pltpu.VMEM((channels, width), bf16),
            pltpu.VMEM((channels, width), f32),
            pltpu.VMEM((n, 2 * mine, width), bf16),
            pltpu.VMEM((n, 2 * mine, width), bf16),
            pltpu.VMEM((n + 1, 2 * most, 2 * width), bf16),
            pltpu.VMEM((n + 1, most, 2 * width), f32),
            pltpu.VMEM((SUBS, n, mine, span), bf16),
            pltpu.VMEM((SUBS, channels, span), bf16),
            pltpu.VMEM((n + 1, 2 * width, 2 * width), bf16),
            pltpu.VMEM((4, channels, feats), bf16),
            pltpu.VMEM((width, channels), bf16),
            pltpu.VMEM((4, width, feats), f32),
            pltpu.VMEM((2, SUBS, span, feats), bf16),
            pltpu.VMEM((2, SUBS, span, feats), bf16),
            pltpu.VMEM((SUBS, span, feats), bf16),
            pltpu.VMEM((SUBS, span, feats), bf16),
            dma((SUBS, PIECES)),
            dma((CHUNKS, 4)),
            dma((5,)),
            dma((CHUNKS, n)),
            dma((CHUNKS, n)),
            dma((CHUNKS, SUBS, n)),
            dma((CHUNKS, SUBS, n)),
            dma((2, SUBS, PIECES)),
            dma((2, SUBS, PIECES)),
            dma((SUBS, PIECES)),
            dma((SUBS, PIECES)),
        ],
        compiler_params=pltpu.CompilerParams(
            collective_id=0, has_side_effects=True, vmem_limit_bytes=40 * 1024 * 1024
        ),
    )(
        signal, pre_gate, post_gate, filter_taps, skip_gain.reshape(channels // 128, 128), out_weight,
        jnp.asarray(freq_tables(n, width)),
    )


def per_device(signal, *rest):
    channels, width = signal.shape
    features = rest[-1].shape[1]
    n, tp = lax.axis_size("ctx"), lax.axis_size("tp")
    fits = n in (2, 4, 8) and tp == 4 and width % 256 == 0
    fits = fits and channels % (4 * n * 16) == 0 and channels % (4 * 128) == 0
    fits = fits and features % (4 * PIECES * 256) == 0
    return (per_device_fused if fits else per_device_generic)(signal, *rest)


def solution(mesh):
    return jax.shard_map(
        per_device,
        mesh=mesh,
        in_specs=(
            P("tp", "ctx"),
            P("tp", "ctx"),
            P("tp", "ctx"),
            P("tp", "ctx"),
            P("tp"),
            P("tp", None),
        ),
        out_specs=P("tp", "ctx"),
        check_vma=False,
    )
```

```python
import functools
import math

import jax
import jax.numpy as jnp
import numpy as np
from jax import lax
from jax.experimental import pallas as pl
from jax.experimental.pallas import tpu as pltpu
from jax.sharding import PartitionSpec as P

f32 = jnp.float32
bf16 = jnp.bfloat16


def freq_tables(blocks, width):
    total = 2 * blocks * width
    place = np.arange(width, dtype=np.int64)
    tables = []
    for k1 in range(blocks + 1):
        angle = (place[:, None] * (k1 + 2 * blocks * place[None, :]) % total) * (2.0 * math.pi / total)
        c, s = np.cos(angle), np.sin(angle)
        tables.append(np.block([[c, -s], [s, c]]))
    return np.stack(tables).astype(jnp.bfloat16)


def weighted(terms):
    total = None
    for coef, part in terms:
        if abs(coef) < 1e-12:
            continue
        value = part if coef == 1.0 else (-part if coef == -1.0 else part * coef)
        total = value if total is None else total + value
    return total


def unit(fn, b, k1, n):
    value = fn(math.pi * (b * k1 % (2 * n)) / n)
    return float(round(value)) if abs(value - round(value)) < 1e-12 else value


def front(n, rows, load, spec):
    width = spec.shape[-1] // 2
    x = [load(b) for b in range(n)]
    even, odd = range(0, n, 2), range(1, n, 2)
    for k1 in range(n // 2 + 1):
        ce = weighted([(unit(math.cos, b, k1, n), x[b]) for b in even])
        co = weighted([(unit(math.cos, b, k1, n), x[b]) for b in odd])
        se = weighted([(unit(math.sin, b, k1, n), x[b]) for b in even])
        so = weighted([(unit(math.sin, b, k1, n), x[b]) for b in odd])
        k2 = n - k1
        if k1 == k2:
            spec[k1, rows, :width] = ce.astype(bf16)
            spec[k1, rows, width:] = (-so).astype(bf16)
            continue
        spec[k1, rows, :width] = (ce + co).astype(bf16)
        spec[k2, rows, :width] = (ce - co).astype(bf16)
        if k1:
            spec[k1, rows, width:] = (-(se + so)).astype(bf16)
            spec[k2, rows, width:] = (se - so).astype(bf16)


def middle(k1, channels, real_only, spec, table, wide):
    width = table.shape[-1] // 2
    depth = width if real_only else 2 * width
    full = jnp.dot(spec[k1, : 2 * channels, :depth], table[k1, :depth, :], preferred_element_type=f32)
    ur, ui = full[:channels, :width], full[:channels, width:]
    hr, hi = full[channels:, :width], full[channels:, width:]
    prod = jnp.concatenate([ur * hr - ui * hi, ur * hi + ui * hr], axis=1).astype(bf16)
    wide[k1, :channels, :depth] = lax.dot_general(
        prod, table[k1, :depth, :], (((1,), (1,)), ((), ())), preferred_element_type=f32
    )


def back(n, rows, wide, store):
    width = wide.shape[-1] // 2
    scale = 1.0 / (2 * n * width)
    re = [wide[k, rows, :width] for k in range(n + 1)]
    im = [None if k in (0, n) else wide[k, rows, width:] for k in range(n + 1)]
    for parity in (0, 1):
        sign = 1.0 if parity == 0 else -1.0
        reals, imags = [], []
        for k in range(n // 2):
            reals.append(re[k] + re[n - k] if parity == 0 else re[k] - re[n - k])
            imags.append(None if k == 0 else (im[k] - im[n - k] if parity == 0 else im[k] + im[n - k]))
        for b in range(parity, n, 2):
            terms = []
            for k in range(n // 2):
                weight = scale if k == 0 else 2.0 * scale
                terms.append((weight * unit(math.cos, b, k, n), reals[k]))
                if k:
                    terms.append((-weight * unit(math.sin, b, k, n), imags[k]))
            if parity == 0:
                terms.append((2.0 * scale * unit(math.cos, b, n // 2, n), re[n // 2]))
            else:
                terms.append((-2.0 * scale * unit(math.sin, b, n // 2, n), im[n // 2]))
            terms = [(c if abs(c) > 1e-9 * scale else 0.0, v) for c, v in terms]
            store(b, weighted([(c / scale, v) for c, v in terms]) * scale)


ROWS = 16


def conv_kernel(n, x_ref, table, y_ref, spec, wide):
    channels = y_ref.shape[1]

    def front_step(i, _):
        rows = pl.ds(pl.multiple_of(i * ROWS, ROWS), ROWS)
        front(n, rows, lambda b: x_ref[b, rows, :].astype(f32), spec)
        return 0

    lax.fori_loop(0, 2 * channels // ROWS, front_step, 0)
    middle(0, channels, True, spec, table, wide)
    middle(n, channels, True, spec, table, wide)

    def middle_step(k1, _):
        middle(k1, channels, False, spec, table, wide)
        return 0

    lax.fori_loop(1, n, middle_step, 0)

    height = min(ROWS, channels)

    def back_step(i, _):
        rows = pl.ds(pl.multiple_of(i * height, height), height)

        def store(b, value):
            y_ref[b, rows, :] = value.astype(bf16)

        back(n, rows, wide, store)
        return 0

    lax.fori_loop(0, channels // height, back_step, 0)


def per_device_generic(signal, pre_gate, post_gate, filter_taps, skip_gain, out_weight):
    channels_here, tokens_here = signal.shape
    n = lax.axis_size("ctx")
    mine = channels_here // n
    gated_input = signal.astype(f32) * pre_gate.astype(f32)
    stacked = jnp.stack([gated_input.astype(bf16), filter_taps.astype(bf16)])
    stacked = stacked.reshape(2, n, mine, tokens_here).transpose(1, 0, 2, 3).reshape(n, 2 * mine, tokens_here)
    blocks = lax.all_to_all(stacked, "ctx", split_axis=0, concat_axis=0, tiled=True)
    table = jnp.asarray(freq_tables(n, tokens_here))
    conv = pl.pallas_call(
        functools.partial(conv_kernel, n),
        out_shape=jax.ShapeDtypeStruct((n, mine, tokens_here), bf16),
        in_specs=[pl.BlockSpec(memory_space=pltpu.VMEM)] * 2,
        out_specs=pl.BlockSpec(memory_space=pltpu.VMEM),
        scratch_shapes=[
            pltpu.VMEM((n + 1, 2 * mine, 2 * tokens_here), bf16),
            pltpu.VMEM((n + 1, mine, 2 * tokens_here), f32),
        ],
        compiler_params=pltpu.CompilerParams(vmem_limit_bytes=48 * 1024 * 1024),
    )(blocks, table)
    conv = lax.all_to_all(conv, "ctx", split_axis=0, concat_axis=0, tiled=True)
    convolved = conv.reshape(channels_here, tokens_here).astype(f32)
    mixed = (post_gate.astype(f32) * (convolved + skip_gain[:, None] * gated_input)).astype(bf16)
    return lax.psum_scatter(
        lax.dot_general(
            out_weight, mixed, (((0,), (0,)), ((), ())), preferred_element_type=f32
        ).astype(bf16),
        "tp",
        scatter_dimension=0,
        tiled=True,
    )


MESH = pl.DeviceIdType.MESH
CHUNKS = 2
SUBS = 2
PIECES = 2


def chunk_sizes(mine):
    return (mine - mine // 4, mine // 4)


def fused_kernel(
    n, sig_hbm, pre_hbm, post_hbm, taps_hbm, skip, weight_hbm, table_hbm, out_any,
    out, sig, pre, post, taps, x_send, x_recv, spec, wide, y_send, y_recv, table, weight, mixed_t, part, a_send, a_recv, c_send, c_recv,
    out_sem, in_sem, load_sem, xs_sem, xr_sem, ys_sem, yr_sem, as_sem, ar_sem, cs_sem, cr_sem,
):
    me = lax.axis_index("ctx")
    tp = lax.axis_index("tp")
    row, core = tp // 2, tp % 2
    partner = row * 2 + (1 - core)
    across = (1 - row) * 2 + core
    channels, width = sig.shape
    sizes = chunk_sizes(channels // n)
    offsets = (0, sizes[0])
    feats = out.shape[0]
    far_peers = [m for m in range(1, n) if 2 * m >= n]
    near_peers = [m for m in range(1, n) if 2 * m < n]
    order = [m for i, far_peer in enumerate(far_peers) for m in [far_peer] + near_peers[i : i + 1]]
    span = width // SUBS

    def peer_of(mask):
        peer, bit = me, 1
        while bit < n:
            if mask // bit % 2:
                peer = peer + bit * (1 - 2 * ((me // bit) % 2))
            bit *= 2
        return peer


    in_loads = []
    for h in range(CHUNKS):
        rows = pl.ds(n * offsets[h], n * sizes[h])
        pairs = ((sig_hbm, sig), (pre_hbm, pre), (taps_hbm, taps), (post_hbm, post))
        in_loads.append(
            [
                pltpu.make_async_copy(source.at[rows], target.at[rows], in_sem.at[h, i])
                for i, (source, target) in enumerate(pairs)
            ]
        )
        for load in in_loads[h][:3]:
            load.start()
    loads = [pltpu.make_async_copy(table_hbm, table, load_sem.at[0])]
    for f in range(4):
        loads.append(
            pltpu.make_async_copy(weight_hbm.at[:, pl.ds(f * feats, feats)], weight.at[f], load_sem.at[1 + f])
        )
    barrier = pltpu.get_barrier_semaphore()
    for d in range(1, n):
        pl.semaphore_signal(barrier, inc=1, device_id={"ctx": peer_of(d)}, device_id_type=MESH)
    pl.semaphore_signal(barrier, inc=1, device_id={"tp": partner}, device_id_type=MESH)
    pl.semaphore_signal(barrier, inc=1, device_id={"tp": across}, device_id_type=MESH)

    def owned(h, peer):
        return pl.ds(pl.multiple_of(n * offsets[h] + peer * sizes[h], 16), sizes[h])

    def pair(h):
        return pl.ds(2 * offsets[h], 2 * sizes[h])

    def gated(rows):
        return sig[rows, :].astype(f32) * pre[rows, :].astype(f32)

    def fill(ref, slot, h, peer):
        rows = owned(h, peer)
        middle_row = 2 * offsets[h] + sizes[h]
        ref[slot, pl.ds(2 * offsets[h], sizes[h]), :] = gated(rows).astype(bf16)
        ref[slot, pl.ds(middle_row, sizes[h]), :] = taps[rows, :].astype(bf16)

    x_copies = {}
    for h in range(CHUNKS):
        for load in in_loads[h][:3]:
            load.wait()
        for d in order:
            fill(x_send, d, h, peer_of(d))
        if h == 0:
            pl.semaphore_wait(barrier, n + 1)
        for d in order:
            copy = pltpu.make_async_remote_copy(
                src_ref=x_send.at[d, pair(h)],
                dst_ref=x_recv.at[me, pair(h)],
                send_sem=xs_sem.at[h, d],
                recv_sem=xr_sem.at[h, d],
                device_id={"ctx": peer_of(d)},
                device_id_type=MESH,
            )
            copy.start()
            x_copies[h, d] = copy
        for load in loads[:1] if h == 0 else loads[1:]:
            load.start()
        in_loads[h][3].start()
    for h in range(CHUNKS):
        fill(x_recv, me, h, me)
    loads[0].wait()

    y_copies = {}
    skip_t = skip[...].T

    def mix(h, t):
        for d in order:
            y_copies[h, t, d].wait_recv()
        y_recv[t, owned(h, me), :] = y_send[t, me, pl.ds(offsets[h], sizes[h])]
        step = 128
        tokens = pl.ds(t * span, span)
        first = n * offsets[h] // step
        for j in range(first, first + n * sizes[h] // step):
            rows = pl.ds(j * step, step)
            gate_in = sig[rows, tokens].astype(f32) * pre[rows, tokens].astype(f32)
            conv = y_recv[t, rows, :].astype(f32)
            value = post[rows, tokens].astype(f32) * (conv + skip_t[:, j : j + 1] * gate_in)
            mixed_t[tokens, rows] = value.T.astype(bf16)

    def send_back(h, t):
        for d in order:
            peer = peer_of(d)
            copy = pltpu.make_async_remote_copy(
                src_ref=y_send.at[t, peer, pl.ds(offsets[h], sizes[h])],
                dst_ref=y_recv.at[t, owned(h, me)],
                send_sem=ys_sem.at[h, t, d],
                recv_sem=yr_sem.at[h, t, d],
                device_id={"ctx": peer},
                device_id_type=MESH,
            )
            copy.start()
            y_copies[h, t, d] = copy

    for h in range(CHUNKS):
        for d in order:
            x_copies[h, d].wait_recv()
        if h == 1:
            send_back(0, 0)
        size = sizes[h]

        def front_step(i, _):
            rows = pl.ds(pl.multiple_of(i * ROWS, ROWS), ROWS)
            source = pl.ds(pl.multiple_of(2 * offsets[h] + i * ROWS, ROWS), ROWS)
            front(n, rows, lambda b: x_recv[b, source, :].astype(f32), spec)
            return 0

        lax.fori_loop(0, 2 * size // ROWS, front_step, 0)
        middle(0, size, True, spec, table, wide)
        middle(n, size, True, spec, table, wide)

        def middle_step(k1, _):
            middle(k1, size, False, spec, table, wide)
            return 0

        lax.fori_loop(1, n, middle_step, 0, unroll=True)

        def back_step(i, _):
            rows = pl.ds(pl.multiple_of(i * ROWS, ROWS), ROWS)
            target = pl.ds(pl.multiple_of(offsets[h] + i * ROWS, ROWS), ROWS)

            def store(b, value):
                for t in range(SUBS):
                    y_send[t, b, target, :] = value[:, t * span : (t + 1) * span].astype(bf16)

            back(n, rows, wide, store)
            return 0

        lax.fori_loop(0, size // ROWS, back_step, 0)
    send_back(1, 0)
    for t in range(1, SUBS):
        send_back(0, t)
        send_back(1, t)

    for load in loads[1:] + [in_loads[h][3] for h in range(CHUNKS)]:
        load.wait()
    tile = 256
    tiles = feats // tile
    head = n * sizes[0]

    def columns(c):
        return pl.ds(pl.multiple_of(c * tile, tile), tile)

    def project(f, tokens, c, lo, hi):
        return jnp.dot(mixed_t[tokens, lo:hi], weight[f, lo:hi, columns(c)], preferred_element_type=f32)

    def each_tile(body, piece=None):
        def step(c, _):
            body(c)
            return 0

        lo, hi = (0, tiles) if piece is None else (piece * tiles // PIECES, (piece + 1) * tiles // PIECES)
        lax.fori_loop(lo, hi, step, 0)

    def reduce_copy(send, recv, send_sems, recv_sems, at, piece, target):
        cut = pl.ds(piece * (feats // PIECES), feats // PIECES)
        copy = pltpu.make_async_remote_copy(
            src_ref=send.at[(*at, slice(None), cut)],
            dst_ref=recv.at[(*at, slice(None), cut)],
            send_sem=send_sems.at[(*at, piece)],
            recv_sem=recv_sems.at[(*at, piece)],
            device_id={"tp": target},
            device_id_type=MESH,
        )
        copy.start()
        return copy

    a_copies, c_copies, out_copies = {}, {}, []
    far = (1 - row) * 2 + (1 - core)
    for t in range(SUBS):
        tokens = pl.ds(t * span, span)
        mix(0, t)

        def early(c):
            part[far, tokens, columns(c)] = project(far, tokens, c, 0, head)
            part[across, tokens, columns(c)] = project(across, tokens, c, 0, head)

        each_tile(early)
        mix(1, t)

        def far_rest(c):
            total = part[far, tokens, columns(c)] + project(far, tokens, c, head, channels)
            a_send[0, t, :, columns(c)] = total.astype(bf16)

        for piece in range(PIECES):
            each_tile(far_rest, piece)
            a_copies[0, t, piece] = reduce_copy(a_send, a_recv, as_sem, ar_sem, (0, t), piece, partner)

        def across_rest(c):
            part[across, tokens, columns(c)] += project(across, tokens, c, head, channels)

        each_tile(across_rest)

        def across_sum(c):
            total = part[across, tokens, columns(c)] + a_recv[0, t, :, columns(c)].astype(f32)
            c_send[t, :, columns(c)] = total.astype(bf16)

        for piece in range(PIECES):
            a_copies[0, t, piece].wait_recv()
            each_tile(across_sum, piece)
            c_copies[t, piece] = reduce_copy(c_send, c_recv, cs_sem, cr_sem, (t,), piece, across)

    def partner_all(c):
        total = project(partner, pl.ds(0, width), c, 0, channels).astype(bf16)
        for t in range(SUBS):
            a_send[1, t, :, columns(c)] = total[t * span : (t + 1) * span]

    for piece in range(PIECES):
        each_tile(partner_all, piece)
        for t in range(SUBS):
            a_copies[1, t, piece] = reduce_copy(a_send, a_recv, as_sem, ar_sem, (1, t), piece, partner)

    def own_all(c):
        part[tp, :, columns(c)] = project(tp, pl.ds(0, width), c, 0, channels)

    each_tile(own_all)
    for t in range(SUBS):
        for piece in range(PIECES):
            a_copies[1, t, piece].wait_recv()
        tokens = pl.ds(t * span, span)

        def own_sum(c):
            part[tp, tokens, columns(c)] += a_recv[1, t, :, columns(c)].astype(f32)

        each_tile(own_sum)
    for t in range(SUBS):
        tokens = pl.ds(t * span, span)

        def finish(c):
            total = part[tp, tokens, columns(c)] + c_recv[t, :, columns(c)].astype(f32)
            out[columns(c), tokens] = total.T.astype(bf16)

        for piece in range(PIECES):
            c_copies[t, piece].wait_recv()
            each_tile(finish, piece)
            rows = pl.ds(piece * (feats // PIECES), feats // PIECES)
            copy = pltpu.make_async_copy(out.at[rows, tokens], out_any.at[rows, tokens], out_sem.at[t, piece])
            copy.start()
            out_copies.append(copy)
    for copy in out_copies:
        copy.wait()
    for group in (x_copies, y_copies, a_copies, c_copies):
        for copy in group.values():
            copy.wait_send()


def per_device_fused(signal, pre_gate, post_gate, filter_taps, skip_gain, out_weight):
    channels, width = signal.shape
    n = lax.axis_size("ctx")
    feats = out_weight.shape[1] // 4
    mine = channels // n
    most = max(chunk_sizes(mine))
    span = width // SUBS
    vmem = pl.BlockSpec(memory_space=pltpu.VMEM)
    hbm = pl.BlockSpec(memory_space=pltpu.HBM)
    dma = pltpu.SemaphoreType.DMA
    return pl.pallas_call(
        functools.partial(fused_kernel, n),
        out_shape=jax.ShapeDtypeStruct((feats, width), bf16),
        in_specs=[hbm] * 4 + [vmem] + [hbm] * 2,
        out_specs=pl.BlockSpec(memory_space=pl.ANY),
        scratch_shapes=[
            pltpu.VMEM((feats, width), bf16),
            pltpu.VMEM((channels, width), bf16),
            pltpu.VMEM((channels, width), bf16),
            pltpu.VMEM((channels, width), bf16),
            pltpu.VMEM((channels, width), f32),
            pltpu.VMEM((n, 2 * mine, width), bf16),
            pltpu.VMEM((n, 2 * mine, width), bf16),
            pltpu.VMEM((n + 1, 2 * most, 2 * width), bf16),
            pltpu.VMEM((n + 1, most, 2 * width), f32),
            pltpu.VMEM((SUBS, n, mine, span), bf16),
            pltpu.VMEM((SUBS, channels, span), bf16),
            pltpu.VMEM((n + 1, 2 * width, 2 * width), bf16),
            pltpu.VMEM((4, channels, feats), bf16),
            pltpu.VMEM((width, channels), bf16),
            pltpu.VMEM((4, width, feats), f32),
            pltpu.VMEM((2, SUBS, span, feats), bf16),
            pltpu.VMEM((2, SUBS, span, feats), bf16),
            pltpu.VMEM((SUBS, span, feats), bf16),
            pltpu.VMEM((SUBS, span, feats), bf16),
            dma((SUBS, PIECES)),
            dma((CHUNKS, 4)),
            dma((5,)),
            dma((CHUNKS, n)),
            dma((CHUNKS, n)),
            dma((CHUNKS, SUBS, n)),
            dma((CHUNKS, SUBS, n)),
            dma((2, SUBS, PIECES)),
            dma((2, SUBS, PIECES)),
            dma((SUBS, PIECES)),
            dma((SUBS, PIECES)),
        ],
        compiler_params=pltpu.CompilerParams(
            collective_id=0, has_side_effects=True, vmem_limit_bytes=56 * 1024 * 1024
        ),
    )(
        signal, pre_gate, post_gate, filter_taps, skip_gain.reshape(channels // 128, 128), out_weight,
        jnp.asarray(freq_tables(n, width)),
    )


def per_device(signal, *rest):
    channels, width = signal.shape
    features = rest[-1].shape[1]
    n, tp = lax.axis_size("ctx"), lax.axis_size("tp")
    fits = n in (2, 4, 8) and tp == 4 and width % 256 == 0
    fits = fits and channels % (4 * n * 16) == 0 and channels % (4 * 128) == 0
    fits = fits and features % (4 * PIECES * 256) == 0
    return (per_device_fused if fits else per_device_generic)(signal, *rest)


def solution(mesh):
    return jax.shard_map(
        per_device,
        mesh=mesh,
        in_specs=(
            P("tp", "ctx"),
            P("tp", "ctx"),
            P("tp", "ctx"),
            P("tp", "ctx"),
            P("tp"),
            P("tp", None),
        ),
        out_specs=P("tp", "ctx"),
        check_vma=False,
    )
```
